512 devices in a mesh: py: 16 (over y, core), pz: 32 (over z, x).
Axes of the slice: x: 4, y: 8, z: 8, core: 2. Of those that a mesh axis runs over, the one named last changes fastest.
Arguments:
- nodal: bfloat16 [16, 14336, 3, 512], P('py', 'pz'), may hold values from -6 to 6
- element_counts: int32 [16, 32], P('py', 'pz'), may hold values from 64 to 448, as said below
- send_slots: int32 [16, 14336], P('py', 'pz'), may hold values from 0 to 511, as said below
- arrival_slots: int32 [16, 16384], P('py', 'pz'), may hold values from 0 to 256, as said below
Outputs:
- spectra: float32 [3, 2, 160, 512, 256], P(None, None, 'py', 'pz')
The draws below stay inside these ranges and needn't reach their ends.
Inputs may be any that keep to these rules, and one draw needn't show every extreme that they name: `element_counts`: within one index of py the counts sum to 8192; some rank of each index of py holds exactly 448 live slots. `send_slots`: the live positions of one rank are distinct; at most 16 of them fall in any one pencil block's range of 16 positions, and in every draw some rank fills a block's range; positions of slots past the count are arbitrary. `arrival_slots`: the value 256 marks a slot that carries nothing, exactly the slots that no live element of the sending rank names; every local index below 256 appears exactly once in each pencil block.
All inputs are finite; a program needn't handle non-finite values.
Results may differ from the reference program's by a relative error of at most 0.0065.
Values may be sent and summed in bfloat16 or wider, within the bound.
A program may use at most 64 MiB of HBM per device.

```python
import math
import jax
import jax.numpy as jnp
import numpy as np
from jax import lax

NODE = 8
EX = 64
KX = 160
YE = 2
LZ = 2
NX = 512
NY = 256
NZ = 512
AVG = 256
PAIR = 8
SLOTS = 16
CAP = 448
N_PY = 16
N_PZ = 32


def band_routing(key):
    subkeys = jax.random.split(key, 7)
    half_count = N_PZ // 2
    load_steps = jax.random.randint(subkeys[0], (half_count,), 0, 3 * PAIR // 4 + 1).at[0].set(3 * PAIR // 4)
    shifts = jnp.concatenate([load_steps, -load_steps])[jax.random.permutation(subkeys[1], N_PZ)]
    ripple_steps = jax.random.randint(subkeys[2], (half_count,), 0, PAIR // 4 + 1).at[0].set(PAIR // 4)
    ripple = jnp.concatenate([ripple_steps, -ripple_steps])[jax.random.permutation(subkeys[3], N_PZ)]
    source = jnp.arange(N_PZ)[:, None]
    target = jnp.arange(N_PZ)[None, :]
    pair_loads = PAIR + shifts[:, None] + ripple[(target - source) % N_PZ]
    counts = jnp.sum(pair_loads, axis=1)
    starts = jnp.cumsum(pair_loads, axis=0) - pair_loads
    column = jnp.arange(SLOTS)
    orders = jax.vmap(lambda subkey: jax.random.permutation(subkey, AVG))(jax.random.split(subkeys[4], N_PZ))
    offsets = starts.T[:, :, None] + column[None, None, :]
    arriving = (column[None, None, :] < pair_loads.T[:, :, None]).reshape(N_PZ, N_PZ * SLOTS)
    picked = jnp.take_along_axis(orders, jnp.minimum(offsets, AVG - 1).reshape(N_PZ, N_PZ * SLOTS), axis=1)
    arrival = jnp.where(arriving, picked, AVG)
    leaving = (column[None, None, :] < pair_loads[:, :, None]).reshape(N_PZ, N_PZ * SLOTS)
    rank_order = jax.vmap(lambda subkey: jax.random.permutation(subkey, N_PZ * SLOTS))(jax.random.split(subkeys[5], N_PZ))
    scores = jnp.where(leaving, rank_order, N_PZ * SLOTS + jnp.arange(N_PZ * SLOTS)[None, :])
    ordered = jnp.argsort(scores, axis=1, stable=True)[:, :CAP]
    filler = jax.random.randint(subkeys[6], (N_PZ, CAP), 0, N_PZ * SLOTS)
    send_rows = jnp.where(jnp.arange(CAP)[None, :] < counts[:, None], ordered, filler)
    return (counts.astype(jnp.int32), send_rows.reshape(-1).astype(jnp.int32), arrival.reshape(-1).astype(jnp.int32))


def routing_tables(key):
    band_keys = jax.random.split(key, N_PY)
    return jax.vmap(band_routing)(band_keys)


def draw_element_counts(key, part):
    tables = routing_tables(key)
    return tables[0]


def draw_send_slots(key, part):
    tables = routing_tables(key)
    return tables[1]


def draw_arrival_slots(key, part):
    tables = routing_tables(key)
    return tables[2]


def levels(stream_key, shape, cuts, smallest, high):
    loudness = 1.0
    for axis_at, shards_of in cuts:
        steps = jax.random.uniform(jax.random.fold_in(jax.random.fold_in(stream_key, 6), axis_at), (shards_of,), jnp.float32, smallest / len(cuts), high / len(cuts))
        loudness = loudness * jnp.repeat(jnp.exp(steps), shape[axis_at] // shards_of).reshape((-1,) + (1,) * (len(shape) - 1 - axis_at))
    return loudness


def noise(rng, dims, spread, bound, pieces=(), kind=jnp.bfloat16):
    entries = jax.random.normal(rng, dims, jnp.float32) * spread
    if len(pieces) > 0:
        entries = levels(rng, dims, pieces, -0.22, 0.18) * entries
    return jnp.clip(entries, min=-bound, max=bound).astype(kind)


def setup_inputs(seed: int = 0) -> dict:
    streams_of = jax.random.split(jax.random.key(seed), 5)
    nodal = noise(streams_of[0], (N_PY, N_PZ * CAP, 3, NODE ** 3), 1.0, 6.0, ((0, 16), (1, 32)))
    element_counts = draw_element_counts(jax.random.fold_in(streams_of[4], 71), 0)
    send_slots = draw_send_slots(jax.random.fold_in(streams_of[4], 71), 0)
    arrival_slots = draw_arrival_slots(jax.random.fold_in(streams_of[4], 71), 0)
    return {"nodal": nodal, "element_counts": element_counts, "send_slots": send_slots, "arrival_slots": arrival_slots}


def lobatto_points(number):
    degree = number - 1
    points = np.cos(np.pi * np.arange(number) / degree)
    for sweeps in range(60):
        older_poly = np.ones(number)
        newer_poly = points.copy()
        for degree_now in range(2, degree + 1):
            older_poly, newer_poly = (newer_poly, ((2 * degree_now - 1) * points * newer_poly - (degree_now - 1) * older_poly) / degree_now)
        points = points - (points * newer_poly - older_poly) / (number * newer_poly)
    return np.sort(points)

def vandermonde(number):
    gauss_points = lobatto_points(number)
    uniform = -1.0 + (2.0 * np.arange(number) + 1.0) / number
    columns_list = []
    for column in range(number):
        same = np.arange(number) == column
        numer = np.where(same[None, :], 1.0, uniform[:, None] - gauss_points[None, :])
        denom = np.where(same, 1.0, gauss_points[column] - gauss_points)
        columns_list.append(np.prod(numer / denom[None, :], axis=1))
    return np.stack(columns_list, axis=1)

def evaluate(coeffs):
    lagrange = jnp.asarray(vandermonde(NODE), dtype=jnp.float32)
    leading = coeffs.shape[:-1]
    cube_values = coeffs.astype(jnp.float32).reshape(leading + (NODE, NODE, NODE))
    highest = lax.Precision.HIGHEST
    cube_values = jnp.einsum('...abc,kc->...abk', cube_values, lagrange, precision=highest)
    cube_values = jnp.einsum('...abk,jb->...ajk', cube_values, lagrange, precision=highest)
    cube_values = jnp.einsum('...ajk,ia->...ijk', cube_values, lagrange, precision=highest)
    return cube_values.reshape(coeffs.shape)

def reference(nodal, element_counts, send_slots, arrival_slots):
    total_slots = N_PZ * SLOTS
    nodes_all = NODE ** 3

    def one_band(inputs):
        band_nodal, band_counts, band_send, band_arrival = inputs
        slot_index = jnp.arange(N_PZ * CAP, dtype=jnp.int32)
        sender = slot_index // CAP
        within = slot_index % CAP
        live = within < band_counts[sender]
        flat_target = jnp.where(live, sender * total_slots + band_send, N_PZ * total_slots).astype(jnp.int32)
        outgoing = jnp.zeros((N_PZ * total_slots, 3, nodes_all), jnp.bfloat16)
        outgoing = outgoing.at[flat_target].set(band_nodal, mode='drop')
        arrived = outgoing.reshape(N_PZ, N_PZ, SLOTS, 3, nodes_all).transpose(1, 0, 2, 3, 4)
        arrived = arrived.reshape(N_PZ * total_slots, 3, nodes_all)
        owners = jnp.arange(N_PZ, dtype=jnp.int32)[:, None]
        local_index = band_arrival.reshape(N_PZ, total_slots)
        placed_index = jnp.where(local_index < AVG, owners * AVG + local_index, N_PZ * AVG).astype(jnp.int32)
        elements = jnp.zeros((N_PZ * AVG, 3, nodes_all), jnp.bfloat16)
        elements = elements.at[placed_index.reshape(-1)].set(arrived, mode='drop')
        values = evaluate(elements).astype(jnp.bfloat16)
        field = values.reshape(N_PZ, LZ, YE, EX, 3, NODE, NODE, NODE).transpose(4, 0, 1, 5, 2, 6, 3, 7)
        field = field.reshape(3, NZ, YE * NODE, NX).astype(jnp.float32)
        spectrum = jnp.fft.rfft(field, axis=-1)[..., :KX] / math.sqrt(NX)
        stacked = jnp.stack([jnp.real(spectrum), jnp.imag(spectrum)], axis=1)
        return stacked.transpose(0, 1, 4, 2, 3).astype(jnp.float32)
    bands = lax.map(one_band, (nodal, element_counts, send_slots, arrival_slots))
    return bands.transpose(1, 2, 3, 4, 0, 5).reshape(3, 2, KX, NZ, NY)
```

```python
import functools
import math

import jax
import jax.numpy as jnp
import ml_dtypes
import numpy as np
from jax import lax
from jax.experimental import pallas as pl
from jax.experimental.pallas import tpu as pltpu
from jax.sharding import PartitionSpec as P

NODE = 8
YE = 2
LZ = 2
BLOCKS = YE * LZ
COMPONENTS = 3
SLOTS = 16
X_RING = 4
MODES = 10
USED = 2 * MODES
PADDED = 32
GROUP = 4
BF16 = jnp.bfloat16
F32 = jnp.float32
MESH = pl.DeviceIdType.MESH


def lobatto_points(number):
    degree = number - 1
    points = np.cos(np.pi * np.arange(number) / degree)
    for sweeps in range(60):
        older_poly = np.ones(number)
        newer_poly = points.copy()
        for degree_now in range(2, degree + 1):
            older_poly, newer_poly = (
                newer_poly,
                ((2 * degree_now - 1) * points * newer_poly - (degree_now - 1) * older_poly)
                / degree_now,
            )
        points = points - (points * newer_poly - older_poly) / (number * newer_poly)
    return np.sort(points)


def vandermonde(number):
    gauss_points = lobatto_points(number)
    uniform = -1.0 + (2.0 * np.arange(number) + 1.0) / number
    columns_list = []
    for column in range(number):
        same = np.arange(number) == column
        numer = np.where(same[None, :], 1.0, uniform[:, None] - gauss_points[None, :])
        denom = np.where(same, 1.0, gauss_points[column] - gauss_points)
        columns_list.append(np.prod(numer / denom[None, :], axis=1))
    return np.stack(columns_list, axis=1)


def fourier_table(bands, elements):
    length = elements * NODE
    wavenumber = np.arange(bands * MODES)[:, None]
    angles = (wavenumber * np.arange(length)[None, :] % length) * (2.0 * np.pi / length)
    dft = np.stack([np.cos(angles), -np.sin(angles)]) / math.sqrt(length)
    dft = dft.reshape(2, bands, MODES, elements, NODE)
    nodes = np.einsum("tikeh,hn->itken", dft, vandermonde(NODE))
    nodes = nodes.reshape(bands, USED, elements, NODE // 2, 2).transpose(4, 0, 1, 3, 2)
    table = np.zeros((2, bands, PADDED, NODE // 2, elements))
    table[:, :, :USED] = nodes
    return table.reshape(2, bands * PADDED, NODE // 2 * elements).astype(ml_dtypes.bfloat16)


def plane_table():
    lagrange = vandermonde(NODE)
    eye = np.eye(2)
    table = np.einsum("ac,bd,q,fu,gv->abquvcfdg", eye, eye, np.ones(2), lagrange, lagrange)
    return table.reshape(BLOCKS * 128, 256).astype(ml_dtypes.bfloat16)


def transfer_kernel(
    n_py, n_pz, nodal, counts, send_slots, arrival_slots, fourier, plane, received,
    nodes, fourier_here, plane_here, pick, place, order, outgoing, arrived, stacked, coeffs,
    load_sem, send_sem, arrive_sem, spread_sem, receive_sem,
):
    me_y = lax.axis_index("py")
    me_z = lax.axis_index("pz")
    z_ring = n_pz // X_RING
    my_plane, my_column = me_z // X_RING, me_z % X_RING
    capacity = nodes.shape[1]
    values = nodes.shape[2]
    elements = place.shape[0] // BLOCKS
    total_slots = n_pz * SLOTS

    barrier = pltpu.get_barrier_semaphore()

    def greet_z(step, carry):
        pl.semaphore_signal(
            barrier, inc=1, device_id={"pz": (me_z + step) % n_pz}, device_id_type=MESH
        )
        return carry

    def greet_y(step, carry):
        pl.semaphore_signal(
            barrier, inc=1, device_id={"py": (me_y + step) % n_py}, device_id_type=MESH
        )
        return carry

    lax.fori_loop(1, n_pz, greet_z, 0)
    lax.fori_loop(1, n_py, greet_y, 0)

    loads = [
        pltpu.make_async_copy(nodal.at[c], nodes.at[c], load_sem.at[c]) for c in range(COMPONENTS)
    ]
    loads.append(pltpu.make_async_copy(fourier, fourier_here, load_sem.at[COMPONENTS]))
    loads.append(pltpu.make_async_copy(plane, plane_here, load_sem.at[COMPONENTS + 1]))
    for load in loads:
        load.start()

    column = lax.broadcasted_iota(jnp.int32, (1, capacity), 1)
    target = jnp.where(column < counts[...], send_slots[...], -1)
    row = lax.broadcasted_iota(jnp.int32, (total_slots, capacity), 0)
    pick[...] = jnp.where(row == target, 1.0, 0.0).astype(BF16)
    old = lax.broadcasted_iota(jnp.int32, (values, values), 0)
    new = lax.broadcasted_iota(jnp.int32, (values, values), 1)
    wanted = (new % 64) * NODE + new // 64
    order[...] = jnp.where(old == wanted, 1.0, 0.0).astype(BF16)

    def pack(c):
        loads[c].wait()
        turned = jnp.dot(nodes[c], order[...], preferred_element_type=F32).astype(BF16)
        packed = jnp.dot(pick[...], turned, preferred_element_type=F32).astype(BF16)
        outgoing[c] = packed.reshape(n_pz, SLOTS, values)

    def send_to(c, plane_step, column_step):
        peer_plane = (my_plane + plane_step + z_ring) % z_ring
        peer = peer_plane * X_RING + (my_column + column_step) % X_RING
        pltpu.make_async_remote_copy(
            src_ref=outgoing.at[c, peer],
            dst_ref=arrived.at[c, me_z],
            send_sem=send_sem.at[c],
            recv_sem=arrive_sem.at[c],
            device_id={"pz": peer},
            device_id_type=MESH,
        ).start()

    def send(c):
        def far(step, carry):
            turn = step // X_RING
            send_to(c, (turn + 2) // 2 * (1 - 2 * (turn % 2)), step % X_RING)
            return carry

        def near(step, carry):
            send_to(c, 0, step)
            return carry

        lax.fori_loop(0, (z_ring - 1) * X_RING, far, 0)
        lax.fori_loop(1, X_RING, near, 0)
        arrived[c, me_z] = outgoing[c, me_z]

    def wait_for(ref, blocks, sem):
        part = ref.at[pl.ds(0, blocks)]
        pltpu.make_async_copy(part, part, sem).wait()

    rows = GROUP * PADDED
    groups = n_py // GROUP

    def transform(c):
        wait_for(arrived.at[c], n_pz - 1, arrive_sem.at[c])
        slots = arrived[c].reshape(total_slots, values)
        placed = jnp.dot(place[...], slots, preferred_element_type=F32).astype(BF16)
        for block in range(BLOCKS):
            for pair in range(NODE // 2):
                stacked[pl.ds(pair * elements, elements), pl.ds(block * 128, 128)] = placed[
                    block * elements : (block + 1) * elements, pair * 128 : (pair + 1) * 128
                ]
        if c == 0:
            loads[COMPONENTS].wait()
            loads[COMPONENTS + 1].wait()

        def group_step(step, carry):
            group = (me_y // GROUP + step) % groups
            here = pl.ds(pl.multiple_of(group * rows, rows), rows)
            even = jnp.dot(fourier_here[0, here], stacked[...], preferred_element_type=F32)
            odd = jnp.dot(fourier_here[1, here], stacked[...], preferred_element_type=F32)
            lane = lax.broadcasted_iota(jnp.int32, even.shape, 1)
            mixed = jnp.where(lane % 128 < 64, even, odd).astype(BF16)
            result = jnp.dot(mixed, plane_here[...], preferred_element_type=F32).astype(BF16)
            coeffs[c, pl.ds(group * GROUP, GROUP)] = result.reshape(GROUP, PADDED, 256)

            def spread(member, inner):
                peer = group * GROUP + (me_y + member) % GROUP

                @pl.when(peer != me_y)
                def _():
                    pltpu.make_async_remote_copy(
                        src_ref=coeffs.at[c, peer],
                        dst_ref=received.at[c, me_y],
                        send_sem=spread_sem.at[c],
                        recv_sem=receive_sem.at[c],
                        device_id={"py": peer},
                        device_id_type=MESH,
                    ).start()

                return inner

            lax.fori_loop(0, GROUP, spread, 0)
            return carry

        lax.fori_loop(0, groups, group_step, 0)
        received[c, me_y] = coeffs[c, me_y]

    pack(0)
    pl.semaphore_wait(barrier, n_pz - 1 + n_py - 1)
    send(0)
    local = lax.broadcasted_iota(jnp.int32, (place.shape[0], total_slots), 0)
    place[...] = jnp.where(local == arrival_slots[...], 1.0, 0.0).astype(BF16)
    for c in range(COMPONENTS):
        if c + 1 < COMPONENTS:
            pack(c + 1)
            send(c + 1)
        transform(c)
    for c in range(COMPONENTS):
        wait_for(outgoing.at[c], n_pz - 1, send_sem.at[c])
        wait_for(coeffs.at[c], n_py - 1, spread_sem.at[c])
        wait_for(received.at[c], n_py - 1, receive_sem.at[c])


def transfer(n_py, n_pz, nodal, counts, send_slots, arrival_slots):
    capacity, values = nodal.shape[1:]
    total_slots = n_pz * SLOTS
    elements = total_slots // 2 // BLOCKS
    fourier = jnp.asarray(fourier_table(n_py, elements))
    plane = jnp.asarray(plane_table())
    vmem = pl.BlockSpec(memory_space=pltpu.VMEM)
    anywhere = pl.BlockSpec(memory_space=pl.ANY)
    return pl.pallas_call(
        functools.partial(transfer_kernel, n_py, n_pz),
        out_shape=jax.ShapeDtypeStruct((COMPONENTS, n_py, PADDED, 256), BF16),
        in_specs=[anywhere, vmem, vmem, vmem, anywhere, anywhere],
        out_specs=vmem,
        scratch_shapes=[
            pltpu.VMEM((COMPONENTS, capacity, values), BF16),
            pltpu.VMEM(fourier.shape, BF16),
            pltpu.VMEM(plane.shape, BF16),
            pltpu.VMEM((total_slots, capacity), BF16),
            pltpu.VMEM((total_slots // 2, total_slots), BF16),
            pltpu.VMEM((values, values), BF16),
            pltpu.VMEM((COMPONENTS, n_pz, SLOTS, values), BF16),
            pltpu.VMEM((COMPONENTS, n_pz, SLOTS, values), BF16),
            pltpu.VMEM((NODE // 2 * elements, BLOCKS * 128), BF16),
            pltpu.VMEM((COMPONENTS, n_py, PADDED, 256), BF16),
            pltpu.SemaphoreType.DMA((COMPONENTS + 2,)),
            pltpu.SemaphoreType.DMA((COMPONENTS,)),
            pltpu.SemaphoreType.DMA((COMPONENTS,)),
            pltpu.SemaphoreType.DMA((COMPONENTS,)),
            pltpu.SemaphoreType.DMA((COMPONENTS,)),
        ],
        compiler_params=pltpu.CompilerParams(
            collective_id=0, has_side_effects=True, vmem_limit_bytes=40 * 1024 * 1024
        ),
    )(nodal, counts, send_slots, arrival_slots, fourier, plane)


def assemble_kernel(received, out, here, spread, load_sem, store_sem):
    bands = received.shape[1]
    granule = lax.broadcasted_iota(jnp.int32, (PADDED, 128), 1) // 16
    loads = [
        pltpu.make_async_copy(received.at[c], here.at[c], load_sem.at[c]) for c in range(COMPONENTS)
    ]
    for load in loads:
        load.start()
    stores = []
    for c in range(COMPONENTS):
        loads[c].wait()
        for half in range(bands // 8):
            for layer in range(2):
                tiles = [
                    here[c, half * 8 + band, :, pl.ds(layer * 128, 128)].astype(F32)
                    for band in range(8)
                ]
                for step in (1, 2, 4):
                    low = granule % (2 * step) < step
                    turned = list(tiles)
                    for at in range(8):
                        if at & step == 0:
                            first, second = tiles[at], tiles[at + step]
                            turned[at] = jnp.where(low, first, pltpu.roll(second, 16 * step, 1))
                            turned[at + step] = jnp.where(
                                low, pltpu.roll(first, 128 - 16 * step, 1), second
                            )
                    tiles = turned
                for at in range(8):
                    rows = pl.ds(layer * 8 + at, USED, stride=16)
                    spread[c, half, rows, :] = tiles[at][:USED]
            store = pltpu.make_async_copy(
                spread.at[c, half], out.at[c, :, pl.ds(half * 128, 128)], store_sem.at[c, half]
            )
            store.start()
            stores.append(store)
    for store in stores:
        store.wait()


def assemble(received):
    n_py = received.shape[1]
    halves = n_py // 8
    return pl.pallas_call(
        assemble_kernel,
        out_shape=jax.ShapeDtypeStruct((COMPONENTS, USED * 16, n_py * 16), F32),
        in_specs=[pl.BlockSpec(memory_space=pl.ANY)],
        out_specs=pl.BlockSpec(memory_space=pl.ANY),
        scratch_shapes=[
            pltpu.VMEM(received.shape, BF16),
            pltpu.VMEM((COMPONENTS, halves, USED * 16, 128), F32),
            pltpu.SemaphoreType.DMA((COMPONENTS,)),
            pltpu.SemaphoreType.DMA((COMPONENTS, halves)),
        ],
        compiler_params=pltpu.CompilerParams(vmem_limit_bytes=24 * 1024 * 1024),
    )(received)


def solution(mesh):
    n_py, n_pz = mesh.shape["py"], mesh.shape["pz"]

    def on_device(nodal, element_counts, send_slots, arrival_slots):
        turned = nodal[0].transpose(1, 0, 2)
        received = transfer(n_py, n_pz, turned, element_counts, send_slots, arrival_slots)
        spectra = assemble(received)
        return spectra.reshape(COMPONENTS, 2, MODES, 16, -1)

    placed = (P("py", "pz", None, None), P("py", "pz"), P("py", "pz"), P("py", "pz"))
    return jax.shard_map(
        on_device,
        mesh=mesh,
        in_specs=placed,
        out_specs=P(None, None, "py", "pz", None),
        check_vma=False,
    )
```

```python
import functools
import math

import jax
import jax.numpy as jnp
import ml_dtypes
import numpy as np
from jax import lax
from jax.experimental import pallas as pl
from jax.experimental.pallas import tpu as pltpu
from jax.sharding import PartitionSpec as P

NODE = 8
YE = 2
LZ = 2
BLOCKS = YE * LZ
COMPONENTS = 3
SLOTS = 16
X_RING = 4
MODES = 10
USED = 2 * MODES
PADDED = 32
GROUP = 4
ROWS = 24
WAVES = 2 * COMPONENTS
WIDTH = NODE**3 // 2
BF16 = jnp.bfloat16
F32 = jnp.float32
MESH = pl.DeviceIdType.MESH


def lobatto_points(number):
    degree = number - 1
    points = np.cos(np.pi * np.arange(number) / degree)
    for sweeps in range(60):
        older_poly = np.ones(number)
        newer_poly = points.copy()
        for degree_now in range(2, degree + 1):
            older_poly, newer_poly = (
                newer_poly,
                ((2 * degree_now - 1) * points * newer_poly - (degree_now - 1) * older_poly)
                / degree_now,
            )
        points = points - (points * newer_poly - older_poly) / (number * newer_poly)
    return np.sort(points)


def vandermonde(number):
    gauss_points = lobatto_points(number)
    uniform = -1.0 + (2.0 * np.arange(number) + 1.0) / number
    columns_list = []
    for column in range(number):
        same = np.arange(number) == column
        numer = np.where(same[None, :], 1.0, uniform[:, None] - gauss_points[None, :])
        denom = np.where(same, 1.0, gauss_points[column] - gauss_points)
        columns_list.append(np.prod(numer / denom[None, :], axis=1))
    return np.stack(columns_list, axis=1)


def fourier_table(bands, elements):
    length = elements * NODE
    wavenumber = np.arange(bands * MODES)[:, None]
    angles = (wavenumber * np.arange(length)[None, :] % length) * (2.0 * np.pi / length)
    dft = np.stack([np.cos(angles), -np.sin(angles)]) / math.sqrt(length)
    dft = dft.reshape(2, bands, MODES, elements, NODE)
    nodes = np.einsum("tikeh,hn->itkne", dft, vandermonde(NODE))
    table = np.zeros((bands, PADDED, NODE, elements))
    table[:, :USED] = nodes.reshape(bands, USED, NODE, elements)
    return table.reshape(bands * PADDED, NODE * elements).astype(ml_dtypes.bfloat16)


def plane_table():
    lagrange = vandermonde(NODE)
    table = np.einsum("fu,gv,hw->uvhwfg", lagrange, lagrange, np.eye(NODE))
    table = table.reshape(NODE**3, NODE, 2, NODE // 2, NODE).transpose(2, 0, 1, 3, 4)
    return table.reshape(2, NODE**3, NODE**3 // 2).astype(ml_dtypes.bfloat16)


def exchange(tiles, index_bit, lane_bit, width):
    lane = lax.broadcasted_iota(jnp.int32, tiles[0].shape, 1)
    shift = lane_bit * width
    low = lane % (2 * shift) < shift
    turned = list(tiles)
    for at in range(len(tiles)):
        if at & index_bit == 0:
            first, second = tiles[at], tiles[at + index_bit]
            turned[at] = jnp.where(low, first, pltpu.roll(second, shift, 1))
            turned[at + index_bit] = jnp.where(low, pltpu.roll(first, 128 - shift, 1), second)
    return turned


def transfer_kernel(
    n_py, n_pz, nodal, counts, send_slots, arrival_slots, fourier, plane, out,
    nodes, counts_here, send_here, arrival_here, fourier_here, plane_here, pick, place,
    outgoing, relayed, arrived, stacked, coeffs, received, ordered, final,
    load_sem, send_sem, relay_sem, forward_sem, arrive_sem, spread_sem, receive_sem, store_sem,
):
    me_y = lax.axis_index("py")
    me_z = lax.axis_index("pz")
    z_ring = n_pz // X_RING
    my_plane, my_column = me_z // X_RING, me_z % X_RING
    capacity = nodes.shape[1]
    elements = place.shape[0] // BLOCKS
    total_slots = n_pz * SLOTS

    barrier = pltpu.get_barrier_semaphore()

    def greet_z(step, carry):
        pl.semaphore_signal(
            barrier, inc=1, device_id={"pz": (me_z + step) % n_pz}, device_id_type=MESH
        )
        return carry

    def greet_y(step, carry):
        pl.semaphore_signal(
            barrier, inc=1, device_id={"py": (me_y + step) % n_py}, device_id_type=MESH
        )
        return carry

    pairs = [
        (send_slots, send_here),
        (counts, counts_here),
        (nodal.at[0], nodes.at[0]),
        (plane, plane_here),
        (arrival_slots, arrival_here),
        (nodal.at[1], nodes.at[1]),
        (nodal.at[2], nodes.at[2]),
        (fourier, fourier_here),
    ]
    loads = [
        pltpu.make_async_copy(source, here, load_sem.at[at])
        for at, (source, here) in enumerate(pairs)
    ]
    for load in loads:
        load.start()
    lax.fori_loop(1, n_pz, greet_z, 0)
    lax.fori_loop(1, n_py, greet_y, 0)

    loads[0].wait()
    loads[1].wait()
    column = lax.broadcasted_iota(jnp.int32, (1, capacity), 1)
    target = jnp.where(column < counts_here[...], send_here[...], -1)
    row = lax.broadcasted_iota(jnp.int32, (total_slots, capacity), 0)
    pick[...] = jnp.where(row == target, 1.0, 0.0).astype(BF16)

    def pack(wave):
        c, half = wave // 2, wave % 2
        turned = jnp.dot(nodes[c], plane_here[half], preferred_element_type=F32).astype(BF16)
        packed = jnp.dot(pick[...], turned, preferred_element_type=F32).astype(BF16)
        outgoing[wave] = packed.reshape(n_pz, SLOTS, WIDTH)

    def peer_at(plane_step, column_step):
        peer_plane = (my_plane + plane_step + z_ring) % z_ring
        return peer_plane * X_RING + (my_column + column_step + X_RING) % X_RING

    def send_to(wave, plane_step, column_step):
        peer = peer_at(plane_step, column_step)
        pltpu.make_async_remote_copy(
            src_ref=outgoing.at[wave, peer],
            dst_ref=arrived.at[wave, me_z],
            send_sem=send_sem.at[wave],
            recv_sem=arrive_sem.at[wave],
            device_id={"pz": peer},
            device_id_type=MESH,
        ).start()

    quarter = z_ring // 4

    def send_opposite(wave):
        def opposite(step, carry):
            way = (1 - step // 2 * 2) * quarter
            pltpu.make_async_remote_copy(
                src_ref=outgoing.at[wave, peer_at(2 * quarter, step)],
                dst_ref=relayed.at[wave, step],
                send_sem=send_sem.at[wave],
                recv_sem=relay_sem.at[wave],
                device_id={"pz": peer_at(way, step)},
                device_id_type=MESH,
            ).start()
            return carry

        lax.fori_loop(0, X_RING, opposite, 0)

    def send(wave):
        def far(step, carry):
            turn = step // X_RING
            send_to(wave, (turn + 2) // 2 * (1 - 2 * (turn % 2)), step % X_RING)
            return carry

        def near(step, carry):
            send_to(wave, 0, step)
            return carry

        lax.fori_loop(0, (z_ring - 2) * X_RING, far, 0)
        lax.fori_loop(1, X_RING, near, 0)
        arrived[wave, me_z] = outgoing[wave, me_z]

    def forward(wave):
        wait_for(relayed.at[wave], X_RING, relay_sem.at[wave])

        def onward(step, carry):
            way = (1 - step // 2 * 2) * quarter
            pltpu.make_async_remote_copy(
                src_ref=relayed.at[wave, step],
                dst_ref=arrived.at[wave, peer_at(-way, -step)],
                send_sem=forward_sem.at[wave],
                recv_sem=arrive_sem.at[wave],
                device_id={"pz": peer_at(way, 0)},
                device_id_type=MESH,
            ).start()
            return carry

        lax.fori_loop(0, X_RING, onward, 0)

    def wait_for(ref, blocks, sem):
        part = ref.at[pl.ds(0, blocks)]
        pltpu.make_async_copy(part, part, sem).wait()

    rows = GROUP * PADDED
    groups = n_py // GROUP

    def transform(wave):
        slots = arrived[wave].reshape(total_slots, WIDTH)
        placed = jnp.dot(place[...], slots, preferred_element_type=F32)
        for quad in range(2):
            tiles = [
                placed[block * elements : (block + 1) * elements, quad * 128 : (quad + 1) * 128]
                for block in range(BLOCKS)
            ]
            tiles = exchange(exchange(tiles, 1, 1, 32), 2, 2, 32)
            for at, tile in enumerate(tiles):
                stacked[pl.ds((quad * 4 + at) * elements, elements), :] = tile.astype(BF16)

        def group_step(step, carry):
            group = (me_y // GROUP + step) % groups
            here = pl.ds(pl.multiple_of(group * rows, rows), rows)
            result = jnp.dot(fourier_here[here], stacked[...], preferred_element_type=F32)
            coeffs[wave, pl.ds(group * GROUP, GROUP)] = result.astype(BF16).reshape(
                GROUP, PADDED, 128
            )

            def spread(member, inner):
                peer = group * GROUP + (me_y + member) % GROUP

                @pl.when(peer != me_y)
                def _():
                    pltpu.make_async_remote_copy(
                        src_ref=coeffs.at[wave, peer],
                        dst_ref=received.at[wave, me_y],
                        send_sem=spread_sem.at[wave],
                        recv_sem=receive_sem.at[wave],
                        device_id={"py": peer},
                        device_id_type=MESH,
                    ).start()

                return inner

            lax.fori_loop(0, GROUP, spread, 0)
            return carry

        lax.fori_loop(0, groups, group_step, 0)
        received[wave, me_y] = coeffs[wave, me_y]

    def put_in_order(wave):
        wait_for(received.at[wave], n_py - 1, receive_sem.at[wave])
        c, half = wave // 2, wave % 2

        def side_step(side, carry):
            tiles = [received[wave, side * 8 + band].astype(F32)[:ROWS] for band in range(8)]
            for index_bit, lane_bit in ((4, 8), (2, 4), (1, 2), (2, 1)):
                tiles = exchange(tiles, index_bit, lane_bit, 8)
            for at in range(8):
                z = at // 4 * 8 + half * 4 + at % 2 * 2 + at // 2 % 2
                ordered[c, side, pl.ds(z, USED, stride=16), :] = tiles[at][:USED]
            return carry

        lax.fori_loop(0, n_py // 8, side_step, 0)

    def store(c):
        for side in range(n_py // 8):
            final[c, :, pl.ds(side * 128, 128)] = ordered[c, side].astype(BF16)
        copy = pltpu.make_async_copy(final.at[c], out.at[c], store_sem.at[c])
        copy.start()
        return copy

    loads[2].wait()
    loads[3].wait()
    pack(0)
    pl.semaphore_wait(barrier, n_pz - 1 + n_py - 1)
    send_opposite(0)
    pack(1)
    send_opposite(1)
    send(0)
    loads[5].wait()
    pack(2)
    send_opposite(2)
    pack(3)
    send_opposite(3)
    forward(0)
    forward(1)
    send(1)
    loads[6].wait()
    pack(4)
    pack(5)
    loads[4].wait()
    local = lax.broadcasted_iota(jnp.int32, (place.shape[0], total_slots), 0)
    place[...] = jnp.where(local == arrival_here[...], 1.0, 0.0).astype(BF16)
    loads[7].wait()
    for wave in range(WAVES):
        wait_for(arrived.at[wave], n_pz - 1, arrive_sem.at[wave])
        if wave + 4 < WAVES:
            send_opposite(wave + 4)
        if wave + 3 < WAVES:
            forward(wave + 2)
            send(wave + 2)
        transform(wave)
        if wave + 3 == WAVES:
            forward(wave + 2)
            send(wave + 2)
        if wave >= 3:
            put_in_order(wave - 3)
    copies = [store(0)]
    put_in_order(3)
    copies.append(store(1))
    put_in_order(4)
    put_in_order(5)
    copies.append(store(2))
    for wave in range(WAVES):
        wait_for(outgoing.at[wave], n_pz - 1, send_sem.at[wave])
        wait_for(relayed.at[wave], X_RING, forward_sem.at[wave])
        wait_for(coeffs.at[wave], n_py - 1, spread_sem.at[wave])
    for copy in copies:
        copy.wait()


def transfer(n_py, n_pz, nodal, counts, send_slots, arrival_slots):
    capacity, values = nodal.shape[1:]
    total_slots = n_pz * SLOTS
    elements = total_slots // 2 // BLOCKS
    fourier = jnp.asarray(fourier_table(n_py, elements))
    plane = jnp.asarray(plane_table())
    anywhere = pl.BlockSpec(memory_space=pl.ANY)
    return pl.pallas_call(
        functools.partial(transfer_kernel, n_py, n_pz),
        out_shape=jax.ShapeDtypeStruct((COMPONENTS, USED * 16, n_py * 16), BF16),
        in_specs=[anywhere] * 6,
        out_specs=anywhere,
        scratch_shapes=[
            pltpu.VMEM((COMPONENTS, capacity, values), BF16),
            pltpu.VMEM(counts.shape, jnp.int32),
            pltpu.VMEM(send_slots.shape, jnp.int32),
            pltpu.VMEM(arrival_slots.shape, jnp.int32),
            pltpu.VMEM(fourier.shape, BF16),
            pltpu.VMEM(plane.shape, BF16),
            pltpu.VMEM((total_slots, capacity), BF16),
            pltpu.VMEM((total_slots // 2, total_slots), BF16),
            pltpu.VMEM((WAVES, n_pz, SLOTS, WIDTH), BF16),
            pltpu.VMEM((WAVES, X_RING, SLOTS, WIDTH), BF16),
            pltpu.VMEM((WAVES, n_pz, SLOTS, WIDTH), BF16),
            pltpu.VMEM((NODE * elements, 128), BF16),
            pltpu.VMEM((WAVES, n_py, PADDED, 128), BF16),
            pltpu.VMEM((WAVES, n_py, PADDED, 128), BF16),
            pltpu.VMEM((COMPONENTS, n_py // 8, USED * 16, 128), F32),
            pltpu.VMEM((COMPONENTS, USED * 16, n_py * 16), BF16),
            pltpu.SemaphoreType.DMA((8,)),
            pltpu.SemaphoreType.DMA((WAVES,)),
            pltpu.SemaphoreType.DMA((WAVES,)),
            pltpu.SemaphoreType.DMA((WAVES,)),
            pltpu.SemaphoreType.DMA((WAVES,)),
            pltpu.SemaphoreType.DMA((WAVES,)),
            pltpu.SemaphoreType.DMA((WAVES,)),
            pltpu.SemaphoreType.DMA((COMPONENTS,)),
        ],
        compiler_params=pltpu.CompilerParams(
            collective_id=0, has_side_effects=True, vmem_limit_bytes=60 * 1024 * 1024
        ),
    )(nodal, counts, send_slots, arrival_slots, fourier, plane)


def solution(mesh):
    n_py, n_pz = mesh.shape["py"], mesh.shape["pz"]

    def on_device(nodal, element_counts, send_slots, arrival_slots):
        turned = nodal[0].transpose(1, 0, 2)
        spectra = transfer(n_py, n_pz, turned, element_counts, send_slots, arrival_slots)
        return spectra.astype(F32).reshape(COMPONENTS, 2, MODES, 16, -1)

    placed = (P("py", "pz", None, None), P("py", "pz"), P("py", "pz"), P("py", "pz"))
    return jax.shard_map(
        on_device,
        mesh=mesh,
        in_specs=placed,
        out_specs=P(None, None, "py", "pz", None),
        check_vma=False,
    )
```

```python
import functools
import math

import jax
import jax.numpy as jnp
import ml_dtypes
import numpy as np
from jax import lax
from jax.experimental import pallas as pl
from jax.experimental.pallas import tpu as pltpu
from jax.sharding import PartitionSpec as P

NODE = 8
YE = 2
LZ = 2
BLOCKS = YE * LZ
COMPONENTS = 3
SLOTS = 16
X_RING = 4
MODES = 10
USED = 2 * MODES
PADDED = 32
GROUP = 4
ROWS = 24
WAVES = 2 * COMPONENTS
WIDTH = NODE**3 // 2
BF16 = jnp.bfloat16
F32 = jnp.float32
MESH = pl.DeviceIdType.MESH


def lobatto_points(number):
    degree = number - 1
    points = np.cos(np.pi * np.arange(number) / degree)
    for sweeps in range(60):
        older_poly = np.ones(number)
        newer_poly = points.copy()
        for degree_now in range(2, degree + 1):
            older_poly, newer_poly = (
                newer_poly,
                ((2 * degree_now - 1) * points * newer_poly - (degree_now - 1) * older_poly)
                / degree_now,
            )
        points = points - (points * newer_poly - older_poly) / (number * newer_poly)
    return np.sort(points)


def vandermonde(number):
    gauss_points = lobatto_points(number)
    uniform = -1.0 + (2.0 * np.arange(number) + 1.0) / number
    columns_list = []
    for column in range(number):
        same = np.arange(number) == column
        numer = np.where(same[None, :], 1.0, uniform[:, None] - gauss_points[None, :])
        denom = np.where(same, 1.0, gauss_points[column] - gauss_points)
        columns_list.append(np.prod(numer / denom[None, :], axis=1))
    return np.stack(columns_list, axis=1)


def fourier_table(bands, elements):
    length = elements * NODE
    wavenumber = np.arange(bands * MODES)[:, None]
    angles = (wavenumber * np.arange(length)[None, :] % length) * (2.0 * np.pi / length)
    dft = np.stack([np.cos(angles), -np.sin(angles)]) / math.sqrt(length)
    dft = dft.reshape(2, bands, MODES, elements, NODE)
    nodes = np.einsum("tikeh,hn->itkne", dft, vandermonde(NODE))
    table = np.zeros((bands, PADDED, NODE, elements))
    table[:, :USED] = nodes.reshape(bands, USED, NODE, elements)
    return table.reshape(bands * PADDED, NODE * elements).astype(ml_dtypes.bfloat16)


def plane_table():
    lagrange = vandermonde(NODE)
    table = np.einsum("fu,gv,hw->uvhwfg", lagrange, lagrange, np.eye(NODE))
    table = table.reshape(NODE**3, NODE, 2, NODE // 2, NODE).transpose(2, 0, 1, 3, 4)
    return table.reshape(2, NODE**3, NODE**3 // 2).astype(ml_dtypes.bfloat16)


def exchange(tiles, index_bit, lane_bit, width):
    lane = lax.broadcasted_iota(jnp.int32, tiles[0].shape, 1)
    shift = lane_bit * width
    low = lane % (2 * shift) < shift
    turned = list(tiles)
    for at in range(len(tiles)):
        if at & index_bit == 0:
            first, second = tiles[at], tiles[at + index_bit]
            turned[at] = jnp.where(low, first, pltpu.roll(second, shift, 1))
            turned[at + index_bit] = jnp.where(low, pltpu.roll(first, 128 - shift, 1), second)
    return turned


def transfer_kernel(
    n_py, n_pz, nodal, counts, send_slots, arrival_slots, fourier, plane, out,
    nodes, counts_here, send_here, arrival_here, fourier_here, plane_here, pick, place,
    outgoing, relayed, arrived, stacked, coeffs, received, ordered,
    load_sem, send_sem, relay_sem, forward_sem, arrive_sem, spread_sem, receive_sem, store_sem,
):
    me_y = lax.axis_index("py")
    me_z = lax.axis_index("pz")
    z_ring = n_pz // X_RING
    my_plane, my_column = me_z // X_RING, me_z % X_RING
    capacity = nodes.shape[1]
    elements = place.shape[0] // BLOCKS
    total_slots = n_pz * SLOTS

    barrier = pltpu.get_barrier_semaphore()

    def greet_z(step, carry):
        pl.semaphore_signal(
            barrier, inc=1, device_id={"pz": (me_z + step) % n_pz}, device_id_type=MESH
        )
        return carry

    def greet_y(step, carry):
        pl.semaphore_signal(
            barrier, inc=1, device_id={"py": (me_y + step) % n_py}, device_id_type=MESH
        )
        return carry

    pairs = [
        (send_slots, send_here),
        (counts, counts_here),
        (nodal.at[0], nodes.at[0]),
        (plane, plane_here),
        (arrival_slots, arrival_here),
        (nodal.at[1], nodes.at[1]),
        (nodal.at[2], nodes.at[2]),
        (fourier, fourier_here),
    ]
    loads = [
        pltpu.make_async_copy(source, here, load_sem.at[at])
        for at, (source, here) in enumerate(pairs)
    ]
    for load in loads:
        load.start()
    lax.fori_loop(1, n_pz, greet_z, 0)
    lax.fori_loop(1, n_py, greet_y, 0)

    loads[0].wait()
    loads[1].wait()
    column = lax.broadcasted_iota(jnp.int32, (1, capacity), 1)
    target = jnp.where(column < counts_here[...], send_here[...], -1)
    row = lax.broadcasted_iota(jnp.int32, (total_slots, capacity), 0)
    pick[...] = jnp.where(row == target, 1.0, 0.0).astype(BF16)

    def pack(wave):
        c, half = wave // 2, wave % 2
        turned = jnp.dot(nodes[c], plane_here[half], preferred_element_type=F32).astype(BF16)
        packed = jnp.dot(pick[...], turned, preferred_element_type=F32).astype(BF16)
        outgoing[wave] = packed.reshape(n_pz, SLOTS, WIDTH)

    def peer_at(plane_step, column_step):
        peer_plane = (my_plane + plane_step + z_ring) % z_ring
        return peer_plane * X_RING + (my_column + column_step + X_RING) % X_RING

    def send_to(wave, plane_step, column_step):
        peer = peer_at(plane_step, column_step)
        pltpu.make_async_remote_copy(
            src_ref=outgoing.at[wave, peer],
            dst_ref=arrived.at[wave, me_z],
            send_sem=send_sem.at[wave],
            recv_sem=arrive_sem.at[wave],
            device_id={"pz": peer},
            device_id_type=MESH,
        ).start()

    quarter = z_ring // 4

    def send_opposite(wave):
        def opposite(step, carry):
            way = (1 - step // 2 * 2) * quarter
            pltpu.make_async_remote_copy(
                src_ref=outgoing.at[wave, peer_at(2 * quarter, step)],
                dst_ref=relayed.at[wave, step],
                send_sem=send_sem.at[wave],
                recv_sem=relay_sem.at[wave],
                device_id={"pz": peer_at(way, step)},
                device_id_type=MESH,
            ).start()
            return carry

        lax.fori_loop(0, X_RING, opposite, 0)

    def send(wave):
        def far(step, carry):
            turn = step % (z_ring - 2)
            side = 1 - (turn + me_y) % 2 * 2
            send_to(wave, side * (turn // 2 + 1), side * (step // (z_ring - 2)))
            return carry

        def near(step, carry):
            send_to(wave, 0, step)
            return carry

        lax.fori_loop(0, (z_ring - 2) * X_RING, far, 0)
        lax.fori_loop(1, X_RING, near, 0)
        arrived[wave, me_z] = outgoing[wave, me_z]

    def forward(wave):
        wait_for(relayed.at[wave], X_RING, relay_sem.at[wave])

        def onward(step, carry):
            way = (1 - step // 2 * 2) * quarter
            pltpu.make_async_remote_copy(
                src_ref=relayed.at[wave, step],
                dst_ref=arrived.at[wave, peer_at(-way, -step)],
                send_sem=forward_sem.at[wave],
                recv_sem=arrive_sem.at[wave],
                device_id={"pz": peer_at(way, 0)},
                device_id_type=MESH,
            ).start()
            return carry

        lax.fori_loop(0, X_RING, onward, 0)

    def wait_for(ref, blocks, sem):
        part = ref.at[pl.ds(0, blocks)]
        pltpu.make_async_copy(part, part, sem).wait()

    rows = GROUP * PADDED
    groups = n_py // GROUP

    def transform(wave):
        slots = arrived[wave].reshape(total_slots, WIDTH)
        placed = jnp.dot(place[...], slots, preferred_element_type=F32)
        for quad in range(2):
            tiles = [
                placed[block * elements : (block + 1) * elements, quad * 128 : (quad + 1) * 128]
                for block in range(BLOCKS)
            ]
            tiles = exchange(exchange(tiles, 1, 1, 32), 2, 2, 32)
            for at, tile in enumerate(tiles):
                stacked[pl.ds((quad * 4 + at) * elements, elements), :] = tile.astype(BF16)

        def group_step(step, carry):
            group = (me_y // GROUP + step) % groups
            here = pl.ds(pl.multiple_of(group * rows, rows), rows)
            result = jnp.dot(fourier_here[here], stacked[...], preferred_element_type=F32)
            coeffs[wave, pl.ds(group * GROUP, GROUP)] = result.astype(BF16).reshape(
                GROUP, PADDED, 128
            )

            def spread(member, inner):
                peer = group * GROUP + (me_y + member) % GROUP

                @pl.when(peer != me_y)
                def _():
                    pltpu.make_async_remote_copy(
                        src_ref=coeffs.at[wave, peer],
                        dst_ref=received.at[wave, me_y],
                        send_sem=spread_sem.at[wave],
                        recv_sem=receive_sem.at[wave],
                        device_id={"py": peer},
                        device_id_type=MESH,
                    ).start()

                return inner

            lax.fori_loop(0, GROUP, spread, 0)
            return carry

        lax.fori_loop(0, groups, group_step, 0)
        received[wave, me_y] = coeffs[wave, me_y]

    def put_in_order(wave):
        wait_for(received.at[wave], n_py - 1, receive_sem.at[wave])
        c, half = wave // 2, wave % 2

        def side_step(side, carry):
            tiles = [received[wave, side * 8 + band].astype(F32)[:ROWS] for band in range(8)]
            for index_bit, lane_bit in ((4, 8), (2, 4), (1, 2), (2, 1)):
                tiles = exchange(tiles, index_bit, lane_bit, 8)
            for at in range(8):
                z = at // 4 * 8 + half * 4 + at % 2 * 2 + at // 2 % 2
                ordered[c, side, pl.ds(z, USED, stride=16), :] = tiles[at][:USED]
            return carry

        lax.fori_loop(0, n_py // 8, side_step, 0)

    def store(c):
        copies = [
            pltpu.make_async_copy(
                ordered.at[c, side], out.at[c, :, pl.ds(side * 128, 128)], store_sem.at[c, side]
            )
            for side in range(n_py // 8)
        ]
        for copy in copies:
            copy.start()
        return copies

    loads[2].wait()
    loads[3].wait()
    pack(0)
    pl.semaphore_wait(barrier, n_pz - 1 + n_py - 1)
    send_opposite(0)
    pack(1)
    send_opposite(1)
    send(0)
    loads[5].wait()
    pack(2)
    send_opposite(2)
    pack(3)
    send_opposite(3)
    forward(0)
    forward(1)
    send(1)
    loads[6].wait()
    pack(4)
    pack(5)
    loads[4].wait()
    local = lax.broadcasted_iota(jnp.int32, (place.shape[0], total_slots), 0)
    place[...] = jnp.where(local == arrival_here[...], 1.0, 0.0).astype(BF16)
    loads[7].wait()
    for wave in range(WAVES):
        wait_for(arrived.at[wave], n_pz - 1, arrive_sem.at[wave])
        if wave + 4 < WAVES:
            send_opposite(wave + 4)
        if wave + 3 < WAVES:
            forward(wave + 2)
            send(wave + 2)
        transform(wave)
        if wave + 3 == WAVES:
            forward(wave + 2)
            send(wave + 2)
        if wave >= 3:
            put_in_order(wave - 3)
    copies = store(0)
    put_in_order(3)
    copies += store(1)
    put_in_order(4)
    put_in_order(5)
    copies += store(2)
    for wave in range(WAVES):
        wait_for(outgoing.at[wave], n_pz - 1, send_sem.at[wave])
        wait_for(relayed.at[wave], X_RING, forward_sem.at[wave])
        wait_for(coeffs.at[wave], n_py - 1, spread_sem.at[wave])
    for copy in copies:
        copy.wait()


def transfer(n_py, n_pz, nodal, counts, send_slots, arrival_slots):
    capacity, values = nodal.shape[1:]
    total_slots = n_pz * SLOTS
    elements = total_slots // 2 // BLOCKS
    fourier = jnp.asarray(fourier_table(n_py, elements))
    plane = jnp.asarray(plane_table())
    anywhere = pl.BlockSpec(memory_space=pl.ANY)
    return pl.pallas_call(
        functools.partial(transfer_kernel, n_py, n_pz),
        out_shape=jax.ShapeDtypeStruct((COMPONENTS, USED * 16, n_py * 16), F32),
        in_specs=[anywhere] * 6,
        out_specs=anywhere,
        scratch_shapes=[
            pltpu.VMEM((COMPONENTS, capacity, values), BF16),
            pltpu.VMEM(counts.shape, jnp.int32),
            pltpu.VMEM(send_slots.shape, jnp.int32),
            pltpu.VMEM(arrival_slots.shape, jnp.int32),
            pltpu.VMEM(fourier.shape, BF16),
            pltpu.VMEM(plane.shape, BF16),
            pltpu.VMEM((total_slots, capacity), BF16),
            pltpu.VMEM((total_slots // 2, total_slots), BF16),
            pltpu.VMEM((WAVES, n_pz, SLOTS, WIDTH), BF16),
            pltpu.VMEM((WAVES, X_RING, SLOTS, WIDTH), BF16),
            pltpu.VMEM((WAVES, n_pz, SLOTS, WIDTH), BF16),
            pltpu.VMEM((NODE * elements, 128), BF16),
            pltpu.VMEM((WAVES, n_py, PADDED, 128), BF16),
            pltpu.VMEM((WAVES, n_py, PADDED, 128), BF16),
            pltpu.VMEM((COMPONENTS, n_py // 8, USED * 16, 128), F32),
            pltpu.SemaphoreType.DMA((8,)),
            pltpu.SemaphoreType.DMA((WAVES,)),
            pltpu.SemaphoreType.DMA((WAVES,)),
            pltpu.SemaphoreType.DMA((WAVES,)),
            pltpu.SemaphoreType.DMA((WAVES,)),
            pltpu.SemaphoreType.DMA((WAVES,)),
            pltpu.SemaphoreType.DMA((WAVES,)),
            pltpu.SemaphoreType.DMA((COMPONENTS, n_py // 8)),
        ],
        compiler_params=pltpu.CompilerParams(
            collective_id=0, has_side_effects=True, vmem_limit_bytes=60 * 1024 * 1024
        ),
    )(nodal, counts, send_slots, arrival_slots, fourier, plane)


def solution(mesh):
    n_py, n_pz = mesh.shape["py"], mesh.shape["pz"]

    def on_device(nodal, element_counts, send_slots, arrival_slots):
        turned = nodal[0].transpose(1, 0, 2)
        spectra = transfer(n_py, n_pz, turned, element_counts, send_slots, arrival_slots)
        return spectra.reshape(COMPONENTS, 2, MODES, 16, -1)

    placed = (P("py", "pz", None, None), P("py", "pz"), P("py", "pz"), P("py", "pz"))
    return jax.shard_map(
        on_device,
        mesh=mesh,
        in_specs=placed,
        out_specs=P(None, None, "py", "pz", None),
        check_vma=False,
    )
```

```python
import functools
import math

import jax
import jax.numpy as jnp
import ml_dtypes
import numpy as np
from jax import lax
from jax.experimental import pallas as pl
from jax.experimental.pallas import tpu as pltpu
from jax.sharding import PartitionSpec as P

NODE = 8
YE = 2
LZ = 2
BLOCKS = YE * LZ
COMPONENTS = 3
SLOTS = 16
X_RING = 4
MODES = 10
USED = 2 * MODES
TILE = 16
LEFT = USED - TILE
GROUP = 8
WAVES = ((0, 0, 2), (1, 0, 2), (2, 0, 1), (2, 1, 1))
PARTS = ((0, 0, 3), (1, 0, 3), (2, 0, 1), (2, 1, 2))
WIDTH = NODE**3 // 2
BF16 = jnp.bfloat16
F32 = jnp.float32
MESH = pl.DeviceIdType.MESH


def lobatto_points(number):
    degree = number - 1
    points = np.cos(np.pi * np.arange(number) / degree)
    for sweeps in range(60):
        older_poly = np.ones(number)
        newer_poly = points.copy()
        for degree_now in range(2, degree + 1):
            older_poly, newer_poly = (
                newer_poly,
                ((2 * degree_now - 1) * points * newer_poly - (degree_now - 1) * older_poly)
                / degree_now,
            )
        points = points - (points * newer_poly - older_poly) / (number * newer_poly)
    return np.sort(points)


def vandermonde(number):
    gauss_points = lobatto_points(number)
    uniform = -1.0 + (2.0 * np.arange(number) + 1.0) / number
    columns_list = []
    for column in range(number):
        same = np.arange(number) == column
        numer = np.where(same[None, :], 1.0, uniform[:, None] - gauss_points[None, :])
        denom = np.where(same, 1.0, gauss_points[column] - gauss_points)
        columns_list.append(np.prod(numer / denom[None, :], axis=1))
    return np.stack(columns_list, axis=1)


def fourier_table(bands, elements):
    length = elements * NODE
    wavenumber = np.arange(bands * MODES)[:, None]
    angles = (wavenumber * np.arange(length)[None, :] % length) * (2.0 * np.pi / length)
    dft = np.stack([np.cos(angles), -np.sin(angles)]) / math.sqrt(length)
    dft = dft.reshape(2, bands, MODES, elements, NODE)
    nodes = np.einsum("tikeh,hn->itkne", dft, vandermonde(NODE))
    nodes = nodes.reshape(bands, USED, NODE, elements)
    table = np.zeros((2, bands, TILE, NODE, elements))
    table[0] = nodes[:, :TILE]
    table[1, :, :LEFT] = nodes[:, TILE:]
    return table.reshape(2, bands * TILE, NODE * elements).astype(ml_dtypes.bfloat16)


def plane_table():
    lagrange = vandermonde(NODE)
    table = np.einsum("fu,gv,hw->uvhwfg", lagrange, lagrange, np.eye(NODE))
    table = table.reshape(NODE**3, NODE, 2, NODE // 2, NODE).transpose(2, 0, 1, 3, 4)
    return table.reshape(2, NODE**3, NODE**3 // 2).astype(ml_dtypes.bfloat16)


def exchange(tiles, index_bit, lane_bit, width):
    lane = lax.broadcasted_iota(jnp.int32, tiles[0].shape, 1)
    shift = lane_bit * width
    low = lane % (2 * shift) < shift
    turned = list(tiles)
    for at in range(len(tiles)):
        if at & index_bit == 0:
            first, second = tiles[at], tiles[at + index_bit]
            turned[at] = jnp.where(low, first, pltpu.roll(second, shift, 1))
            turned[at + index_bit] = jnp.where(low, pltpu.roll(first, 128 - shift, 1), second)
    return turned


def transfer_kernel(
    n_py, n_pz, nodal, counts, send_slots, arrival_slots, fourier, plane, out,
    nodes, counts_here, send_here, arrival_here, fourier_here, plane_here, pick, place,
    outgoing, relayed, arrived, stacked, leftover, coeffs, received,
    load_sem, send_sem, relay_sem, forward_sem, arrive_sem, spread_sem, receive_sem,
):
    me_y = lax.axis_index("py")
    me_z = lax.axis_index("pz")
    z_ring = n_pz // X_RING
    my_plane, my_column = me_z // X_RING, me_z % X_RING
    capacity = nodes.shape[1]
    elements = place.shape[0] // BLOCKS
    total_slots = n_pz * SLOTS

    barrier = pltpu.get_barrier_semaphore()

    def greet_z(step, carry):
        pl.semaphore_signal(
            barrier, inc=1, device_id={"pz": (me_z + step) % n_pz}, device_id_type=MESH
        )
        return carry

    def greet_y(step, carry):
        pl.semaphore_signal(
            barrier, inc=1, device_id={"py": (me_y + step) % n_py}, device_id_type=MESH
        )
        return carry

    pairs = [
        (send_slots, send_here),
        (counts, counts_here),
        (nodal.at[0], nodes.at[0]),
        (plane, plane_here),
        (arrival_slots, arrival_here),
        (nodal.at[1], nodes.at[1]),
        (nodal.at[2], nodes.at[2]),
        (fourier, fourier_here),
    ]
    loads = [
        pltpu.make_async_copy(source, here, load_sem.at[at])
        for at, (source, here) in enumerate(pairs)
    ]
    for load in loads:
        load.start()
    lax.fori_loop(1, n_pz, greet_z, 0)
    lax.fori_loop(1, n_py, greet_y, 0)

    loads[0].wait()
    loads[1].wait()
    column = lax.broadcasted_iota(jnp.int32, (1, capacity), 1)
    target = jnp.where(column < counts_here[...], send_here[...], -1)
    row = lax.broadcasted_iota(jnp.int32, (total_slots, capacity), 0)
    pick[...] = jnp.where(row == target, 1.0, 0.0).astype(BF16)

    def pack(c):
        for half in range(2):
            turned = jnp.dot(nodes[c], plane_here[half], preferred_element_type=F32).astype(BF16)
            packed = jnp.dot(pick[...], turned, preferred_element_type=F32).astype(BF16)
            outgoing[c, :, half] = packed.reshape(n_pz, SLOTS, WIDTH)

    def peer_at(plane_step, column_step):
        peer_plane = (my_plane + plane_step + z_ring) % z_ring
        return peer_plane * X_RING + (my_column + column_step + X_RING) % X_RING

    def block(ref, wave, device):
        c, first, number = WAVES[wave]
        return ref.at[c, device, pl.ds(first, number)]

    def piece(ref, wave, device):
        c, first, number = PARTS[wave]
        return ref.at[c, device, pl.ds(first, number)]

    def wait_for(part, sem):
        pltpu.make_async_copy(part, part, sem).wait()

    def send_to(wave, plane_step, column_step):
        peer = peer_at(plane_step, column_step)
        pltpu.make_async_remote_copy(
            src_ref=block(outgoing, wave, peer),
            dst_ref=block(arrived, wave, me_z),
            send_sem=send_sem.at[wave],
            recv_sem=arrive_sem.at[wave],
            device_id={"pz": peer},
            device_id_type=MESH,
        ).start()

    quarter = z_ring // 4

    def send_opposite(wave):
        def opposite(step, carry):
            way = (1 - step % 2 * 2) * quarter
            pltpu.make_async_remote_copy(
                src_ref=block(outgoing, wave, peer_at(2 * quarter, step)),
                dst_ref=block(relayed, wave, step),
                send_sem=send_sem.at[wave],
                recv_sem=relay_sem.at[wave],
                device_id={"pz": peer_at(way, step)},
                device_id_type=MESH,
            ).start()
            return carry

        lax.fori_loop(0, X_RING, opposite, 0)

    def send(wave):
        def far(step, carry):
            turn = step % (z_ring - 2)
            side = 1 - (turn + me_y) % 2 * 2
            send_to(wave, side * (turn // 2 + 1), side * (step // (z_ring - 2)))
            return carry

        def near(step, carry):
            send_to(wave, 0, step)
            return carry

        lax.fori_loop(1, X_RING, near, 0)
        lax.fori_loop(0, (z_ring - 2) * X_RING, far, 0)
        c, first, number = WAVES[wave]
        for half in range(first, first + number):
            arrived[c, me_z, half] = outgoing[c, me_z, half]

    def forward(wave):
        wait_for(block(relayed, wave, pl.ds(0, X_RING)), relay_sem.at[wave])

        def onward(step, carry):
            way = (1 - step % 2 * 2) * quarter
            pltpu.make_async_remote_copy(
                src_ref=block(relayed, wave, step),
                dst_ref=block(arrived, wave, peer_at(-way, -step)),
                send_sem=forward_sem.at[wave],
                recv_sem=arrive_sem.at[wave],
                device_id={"pz": peer_at(way, 0)},
                device_id_type=MESH,
            ).start()
            return carry

        lax.fori_loop(0, X_RING, onward, 0)

    def receive(wave):
        wait_for(block(arrived, wave, pl.ds(0, n_pz - 1)), arrive_sem.at[wave])

    rows = GROUP * TILE
    groups = n_py // GROUP

    def transform(c, half):
        slots = arrived[c, :, half].reshape(total_slots, WIDTH)
        placed = jnp.dot(place[...], slots, preferred_element_type=F32)
        for quad in range(2):
            tiles = [
                placed[at * elements : (at + 1) * elements, quad * 128 : (quad + 1) * 128]
                for at in range(BLOCKS)
            ]
            tiles = exchange(exchange(tiles, 1, 1, 32), 2, 2, 32)
            for at, tile in enumerate(tiles):
                stacked[pl.ds((quad * 4 + at) * elements, elements), :] = tile.astype(BF16)

        def group_step(step, carry):
            here = pl.ds(pl.multiple_of(step * rows, rows), rows)
            members = pl.ds(step * GROUP, GROUP)
            result = jnp.dot(fourier_here[0, here], stacked[...], preferred_element_type=F32)
            coeffs[c, members, half] = result.astype(BF16).reshape(GROUP, TILE, 128)
            rest = jnp.dot(fourier_here[1, here], stacked[...], preferred_element_type=F32)
            if half == 0:
                leftover[here] = rest
            else:
                both = leftover[here] + pltpu.roll(rest, LEFT, 0)
                coeffs[c, members, 2] = both.astype(BF16).reshape(GROUP, TILE, 128)
            return carry

        lax.fori_loop(0, groups, group_step, 0)

    def spread(wave):
        c, first, number = PARTS[wave]
        for part in range(first, first + number):
            received[c, me_y, part] = coeffs[c, me_y, part]

        def spread_to(step, carry):
            peer = (me_y + (step + 1) // 2 * (1 - step % 2 * 2) + n_py) % n_py
            pltpu.make_async_remote_copy(
                src_ref=piece(coeffs, wave, peer),
                dst_ref=piece(received, wave, me_y),
                send_sem=spread_sem.at[wave],
                recv_sem=receive_sem.at[wave],
                device_id={"py": peer},
                device_id_type=MESH,
            ).start()
            return carry

        lax.fori_loop(1, n_py, spread_to, 0)

    def gather(wave):
        wait_for(piece(received, wave, pl.ds(0, n_py - 1)), receive_sem.at[wave])

    def put_in_order(c, part):
        def side_step(side, carry):
            tiles = [received[c, side * 8 + band, part].astype(F32) for band in range(8)]
            if part == 2:
                tiles = [tile[: 2 * LEFT] for tile in tiles]
            for index_bit, lane_bit in ((4, 8), (2, 4), (1, 2), (2, 1)):
                tiles = exchange(tiles, index_bit, lane_bit, 8)
            for at in range(8):
                z = at // 4 * 8 + at % 2 * 2 + at // 2 % 2
                if part == 2:
                    for half in range(2):
                        here = pl.ds(TILE * 16 + half * 4 + z, LEFT, stride=16)
                        out[c, side, here, :] = tiles[at][half * LEFT : (half + 1) * LEFT]
                else:
                    out[c, side, pl.ds(part * 4 + z, TILE, stride=16), :] = tiles[at]
            return carry

        lax.fori_loop(0, n_py // 8, side_step, 0)

    loads[2].wait()
    loads[3].wait()
    pack(0)
    pl.semaphore_wait(barrier, n_pz - 1 + n_py - 1)
    send_opposite(0)
    loads[5].wait()
    pack(1)
    send_opposite(1)
    send(0)
    loads[6].wait()
    pack(2)
    send_opposite(2)
    send_opposite(3)
    forward(0)
    forward(1)
    send(1)
    loads[4].wait()
    local = lax.broadcasted_iota(jnp.int32, (place.shape[0], total_slots), 0)
    place[...] = jnp.where(local == arrival_here[...], 1.0, 0.0).astype(BF16)
    loads[7].wait()
    receive(0)
    forward(2)
    send(2)
    transform(0, 0)
    transform(0, 1)
    spread(0)
    receive(1)
    transform(1, 0)
    transform(1, 1)
    spread(1)
    forward(3)
    send(3)
    receive(2)
    transform(2, 0)
    spread(2)
    gather(0)
    for part in range(3):
        put_in_order(0, part)
    receive(3)
    transform(2, 1)
    spread(3)
    gather(1)
    for part in range(3):
        put_in_order(1, part)
    gather(2)
    put_in_order(2, 0)
    gather(3)
    put_in_order(2, 1)
    put_in_order(2, 2)
    for wave in range(len(WAVES)):
        wait_for(block(outgoing, wave, pl.ds(0, n_pz - 1)), send_sem.at[wave])
        wait_for(block(relayed, wave, pl.ds(0, X_RING)), forward_sem.at[wave])
        wait_for(piece(coeffs, wave, pl.ds(0, n_py - 1)), spread_sem.at[wave])


def transfer(n_py, n_pz, nodal, counts, send_slots, arrival_slots):
    capacity, values = nodal.shape[1:]
    total_slots = n_pz * SLOTS
    elements = total_slots // 2 // BLOCKS
    fourier = jnp.asarray(fourier_table(n_py, elements))
    plane = jnp.asarray(plane_table())
    remote = pl.BlockSpec(memory_space=pltpu.HBM)
    here = functools.partial(pltpu.with_memory_space_constraint, memory_space=pltpu.HBM)
    return pl.pallas_call(
        functools.partial(transfer_kernel, n_py, n_pz),
        out_shape=jax.ShapeDtypeStruct((COMPONENTS, n_py // 8, USED * 16, 128), F32),
        in_specs=[remote] * 6,
        out_specs=pl.BlockSpec(memory_space=pltpu.VMEM),
        scratch_shapes=[
            pltpu.VMEM((COMPONENTS, capacity, values), BF16),
            pltpu.VMEM(counts.shape, jnp.int32),
            pltpu.VMEM(send_slots.shape, jnp.int32),
            pltpu.VMEM(arrival_slots.shape, jnp.int32),
            pltpu.VMEM(fourier.shape, BF16),
            pltpu.VMEM(plane.shape, BF16),
            pltpu.VMEM((total_slots, capacity), BF16),
            pltpu.VMEM((total_slots // 2, total_slots), BF16),
            pltpu.VMEM((COMPONENTS, n_pz, 2, SLOTS, WIDTH), BF16),
            pltpu.VMEM((COMPONENTS, X_RING, 2, SLOTS, WIDTH), BF16),
            pltpu.VMEM((COMPONENTS, n_pz, 2, SLOTS, WIDTH), BF16),
            pltpu.VMEM((NODE * elements, 128), BF16),
            pltpu.VMEM((n_py * TILE, 128), F32),
            pltpu.VMEM((COMPONENTS, n_py, 3, TILE, 128), BF16),
            pltpu.VMEM((COMPONENTS, n_py, 3, TILE, 128), BF16),
            pltpu.SemaphoreType.DMA((8,)),
            *[pltpu.SemaphoreType.DMA((len(WAVES),)) for _ in range(6)],
        ],
        compiler_params=pltpu.CompilerParams(
            collective_id=0, has_side_effects=True, vmem_limit_bytes=40 * 1024 * 1024
        ),
    )(
        here(nodal), counts, here(send_slots), here(arrival_slots), here(fourier), here(plane)
    )


def write_kernel(spectra, out, sem):
    copies = [
        pltpu.make_async_copy(
            spectra.at[c, side], out.at[c, :, pl.ds(side * 128, 128)], sem.at[c, side]
        )
        for c in range(COMPONENTS)
        for side in range(spectra.shape[1])
    ]
    for copy in copies:
        copy.start()
    for copy in copies:
        copy.wait()


def write(spectra):
    sides, rows = spectra.shape[1:3]
    anywhere = pl.BlockSpec(memory_space=pl.ANY)
    return pl.pallas_call(
        write_kernel,
        out_shape=jax.ShapeDtypeStruct((COMPONENTS, rows, sides * 128), F32),
        in_specs=[anywhere],
        out_specs=anywhere,
        scratch_shapes=[pltpu.SemaphoreType.DMA((COMPONENTS, sides))],
        compiler_params=pltpu.CompilerParams(vmem_limit_bytes=40 * 1024 * 1024),
    )(spectra)


def solution(mesh):
    n_py, n_pz = mesh.shape["py"], mesh.shape["pz"]

    def on_device(nodal, element_counts, send_slots, arrival_slots):
        turned = nodal[0].transpose(1, 0, 2)
        spectra = transfer(n_py, n_pz, turned, element_counts, send_slots, arrival_slots)
        return write(spectra).reshape(COMPONENTS, 2, MODES, 16, -1)

    placed = (P("py", "pz", None, None), P("py", "pz"), P("py", "pz"), P("py", "pz"))
    return jax.shard_map(
        on_device,
        mesh=mesh,
        in_specs=placed,
        out_specs=P(None, None, "py", "pz", None),
        check_vma=False,
    )
```

```python
import functools
import math

import jax
import jax.numpy as jnp
import ml_dtypes
import numpy as np
from jax import lax
from jax.experimental import pallas as pl
from jax.experimental.pallas import tpu as pltpu
from jax.sharding import PartitionSpec as P

NODE = 8
YE = 2
LZ = 2
BLOCKS = YE * LZ
COMPONENTS = 3
SLOTS = 16
X_RING = 4
MODES = 10
USED = 2 * MODES
TILE = 16
LEFT = USED - TILE
GROUP = 8
WAVES = ((0, 0, 2), (1, 0, 2), (2, 0, 1), (2, 1, 1))
PARTS = ((0, 0, 3), (1, 0, 3), (2, 0, 1), (2, 1, 2))
WIDTH = NODE**3 // 2
BF16 = jnp.bfloat16
F32 = jnp.float32
MESH = pl.DeviceIdType.MESH


def lobatto_points(number):
    degree = number - 1
    points = np.cos(np.pi * np.arange(number) / degree)
    for sweeps in range(60):
        older_poly = np.ones(number)
        newer_poly = points.copy()
        for degree_now in range(2, degree + 1):
            older_poly, newer_poly = (
                newer_poly,
                ((2 * degree_now - 1) * points * newer_poly - (degree_now - 1) * older_poly)
                / degree_now,
            )
        points = points - (points * newer_poly - older_poly) / (number * newer_poly)
    return np.sort(points)


def vandermonde(number):
    gauss_points = lobatto_points(number)
    uniform = -1.0 + (2.0 * np.arange(number) + 1.0) / number
    columns_list = []
    for column in range(number):
        same = np.arange(number) == column
        numer = np.where(same[None, :], 1.0, uniform[:, None] - gauss_points[None, :])
        denom = np.where(same, 1.0, gauss_points[column] - gauss_points)
        columns_list.append(np.prod(numer / denom[None, :], axis=1))
    return np.stack(columns_list, axis=1)


def fourier_table(bands, elements):
    length = elements * NODE
    wavenumber = np.arange(bands * MODES)[:, None]
    angles = (wavenumber * np.arange(length)[None, :] % length) * (2.0 * np.pi / length)
    dft = np.stack([np.cos(angles), -np.sin(angles)]) / math.sqrt(length)
    dft = dft.reshape(2, bands, MODES, elements, NODE)
    nodes = np.einsum("tikeh,hn->itkne", dft, vandermonde(NODE))
    nodes = nodes.reshape(bands, USED, NODE, elements)
    table = np.zeros((2, bands, TILE, NODE, elements))
    table[0] = nodes[:, :TILE]
    table[1, :, :LEFT] = nodes[:, TILE:]
    return table.reshape(2, bands * TILE, NODE * elements).astype(ml_dtypes.bfloat16)


def plane_table():
    lagrange = vandermonde(NODE)
    table = np.einsum("fu,gv,hw->uvhwfg", lagrange, lagrange, np.eye(NODE))
    table = table.reshape(NODE**3, NODE, 2, NODE // 2, NODE).transpose(2, 0, 1, 3, 4)
    return table.reshape(2, NODE**3, NODE**3 // 2).astype(ml_dtypes.bfloat16)


def exchange(tiles, index_bit, lane_bit, width):
    lane = lax.broadcasted_iota(jnp.int32, tiles[0].shape, 1)
    shift = lane_bit * width
    low = lane % (2 * shift) < shift
    turned = list(tiles)
    for at in range(len(tiles)):
        if at & index_bit == 0:
            first, second = tiles[at], tiles[at + index_bit]
            turned[at] = jnp.where(low, first, pltpu.roll(second, shift, 1))
            turned[at + index_bit] = jnp.where(low, pltpu.roll(first, 128 - shift, 1), second)
    return turned


def transfer_kernel(
    n_py, n_pz, nodal, counts, send_slots, arrival_slots, fourier, plane, out,
    nodes, counts_here, send_here, arrival_here, fourier_here, plane_here, pick, place,
    outgoing, relayed, arrived, stacked, leftover, coeffs, received,
    load_sem, send_sem, relay_sem, forward_sem, arrive_sem, spread_sem, receive_sem,
):
    me_y = lax.axis_index("py")
    me_z = lax.axis_index("pz")
    z_ring = n_pz // X_RING
    my_plane, my_column = me_z // X_RING, me_z % X_RING
    capacity = nodes.shape[1]
    elements = place.shape[0] // BLOCKS
    total_slots = n_pz * SLOTS

    barrier = pltpu.get_barrier_semaphore()

    def greet_z(step, carry):
        pl.semaphore_signal(
            barrier, inc=1, device_id={"pz": (me_z + step) % n_pz}, device_id_type=MESH
        )
        return carry

    def greet_y(step, carry):
        pl.semaphore_signal(
            barrier, inc=1, device_id={"py": (me_y + step) % n_py}, device_id_type=MESH
        )
        return carry

    pairs = [
        (send_slots, send_here),
        (counts, counts_here),
        (nodal.at[0], nodes.at[0]),
        (plane, plane_here),
        (arrival_slots, arrival_here),
        (nodal.at[1], nodes.at[1]),
        (nodal.at[2], nodes.at[2]),
        (fourier, fourier_here),
    ]
    loads = [
        pltpu.make_async_copy(source, here, load_sem.at[at])
        for at, (source, here) in enumerate(pairs)
    ]
    for load in loads:
        load.start()
    lax.fori_loop(1, n_pz, greet_z, 0)
    lax.fori_loop(1, n_py, greet_y, 0)

    loads[0].wait()
    loads[1].wait()
    column = lax.broadcasted_iota(jnp.int32, (1, capacity), 1)
    target = jnp.where(column < counts_here[...], send_here[...], -1)
    row = lax.broadcasted_iota(jnp.int32, (total_slots, capacity), 0)
    pick[...] = jnp.where(row == target, 1.0, 0.0).astype(BF16)

    def pack(c):
        for half in range(2):
            turned = jnp.dot(nodes[c], plane_here[half], preferred_element_type=F32).astype(BF16)
            packed = jnp.dot(pick[...], turned, preferred_element_type=F32).astype(BF16)
            outgoing[c, :, half] = packed.reshape(n_pz, SLOTS, WIDTH)

    def peer_at(plane_step, column_step):
        peer_plane = (my_plane + plane_step + z_ring) % z_ring
        return peer_plane * X_RING + (my_column + column_step + X_RING) % X_RING

    def block(ref, wave, device):
        c, first, number = WAVES[wave]
        return ref.at[c, device, pl.ds(first, number)]

    def piece(ref, wave, device):
        c, first, number = PARTS[wave]
        return ref.at[c, device, pl.ds(first, number)]

    def wait_for(part, sem):
        pltpu.make_async_copy(part, part, sem).wait()

    def send_to(wave, plane_step, column_step):
        peer = peer_at(plane_step, column_step)
        pltpu.make_async_remote_copy(
            src_ref=block(outgoing, wave, peer),
            dst_ref=block(arrived, wave, me_z),
            send_sem=send_sem.at[wave],
            recv_sem=arrive_sem.at[wave],
            device_id={"pz": peer},
            device_id_type=MESH,
        ).start()

    quarter = z_ring // 4

    def send_opposite(wave):
        def opposite(step, carry):
            way = (1 - step % 2 * 2) * quarter
            pltpu.make_async_remote_copy(
                src_ref=block(outgoing, wave, peer_at(2 * quarter, step)),
                dst_ref=block(relayed, wave, step),
                send_sem=send_sem.at[wave],
                recv_sem=relay_sem.at[wave],
                device_id={"pz": peer_at(way, step)},
                device_id_type=MESH,
            ).start()
            return carry

        lax.fori_loop(0, X_RING, opposite, 0)

    def send(wave):
        def far(step, carry):
            side = 1 - (step + me_y) % 2 * 2
            pair = step // 2
            send_to(wave, side * (pair % (z_ring // 2 - 1) + 1), side * (pair % X_RING))
            return carry

        def near(step, carry):
            send_to(wave, 0, step)
            return carry

        lax.fori_loop(1, X_RING, near, 0)
        lax.fori_loop(0, (z_ring - 2) * X_RING, far, 0)
        c, first, number = WAVES[wave]
        for half in range(first, first + number):
            arrived[c, me_z, half] = outgoing[c, me_z, half]

    def forward(wave):
        wait_for(block(relayed, wave, pl.ds(0, X_RING)), relay_sem.at[wave])

        def onward(step, carry):
            way = (1 - step % 2 * 2) * quarter
            pltpu.make_async_remote_copy(
                src_ref=block(relayed, wave, step),
                dst_ref=block(arrived, wave, peer_at(-way, -step)),
                send_sem=forward_sem.at[wave],
                recv_sem=arrive_sem.at[wave],
                device_id={"pz": peer_at(way, 0)},
                device_id_type=MESH,
            ).start()
            return carry

        lax.fori_loop(0, X_RING, onward, 0)

    def receive(wave):
        wait_for(block(arrived, wave, pl.ds(0, n_pz - 1)), arrive_sem.at[wave])

    rows = GROUP * TILE
    groups = n_py // GROUP

    def transform(c, half):
        slots = arrived[c, :, half].reshape(total_slots, WIDTH)
        placed = jnp.dot(place[...], slots, preferred_element_type=F32)
        for quad in range(2):
            tiles = [
                placed[at * elements : (at + 1) * elements, quad * 128 : (quad + 1) * 128]
                for at in range(BLOCKS)
            ]
            tiles = exchange(exchange(tiles, 1, 1, 32), 2, 2, 32)
            for at, tile in enumerate(tiles):
                stacked[pl.ds((quad * 4 + at) * elements, elements), :] = tile.astype(BF16)

        def group_step(step, carry):
            here = pl.ds(pl.multiple_of(step * rows, rows), rows)
            members = pl.ds(step * GROUP, GROUP)
            result = jnp.dot(fourier_here[0, here], stacked[...], preferred_element_type=F32)
            coeffs[c, members, half] = result.astype(BF16).reshape(GROUP, TILE, 128)
            rest = jnp.dot(fourier_here[1, here], stacked[...], preferred_element_type=F32)
            if half == 0:
                leftover[here] = rest
            else:
                both = leftover[here] + pltpu.roll(rest, LEFT, 0)
                coeffs[c, members, 2] = both.astype(BF16).reshape(GROUP, TILE, 128)
            return carry

        lax.fori_loop(0, groups, group_step, 0)

    def spread(wave):
        c, first, number = PARTS[wave]
        for part in range(first, first + number):
            received[c, me_y, part] = coeffs[c, me_y, part]

        def spread_to(step, carry):
            peer = (me_y + (step + 1) // 2 * (1 - step % 2 * 2) + n_py) % n_py
            pltpu.make_async_remote_copy(
                src_ref=piece(coeffs, wave, peer),
                dst_ref=piece(received, wave, me_y),
                send_sem=spread_sem.at[wave],
                recv_sem=receive_sem.at[wave],
                device_id={"py": peer},
                device_id_type=MESH,
            ).start()
            return carry

        lax.fori_loop(1, n_py, spread_to, 0)

    def gather(wave):
        wait_for(piece(received, wave, pl.ds(0, n_py - 1)), receive_sem.at[wave])

    def put_in_order(c, part):
        def side_step(side, carry):
            tiles = [received[c, side * 8 + band, part].astype(F32) for band in range(8)]
            if part == 2:
                tiles = [tile[: 2 * LEFT] for tile in tiles]
            for index_bit, lane_bit in ((4, 8), (2, 4), (1, 2), (2, 1)):
                tiles = exchange(tiles, index_bit, lane_bit, 8)
            for at in range(8):
                z = at // 4 * 8 + at % 2 * 2 + at // 2 % 2
                if part == 2:
                    for half in range(2):
                        here = pl.ds(TILE * 16 + half * 4 + z, LEFT, stride=16)
                        out[c, side, here, :] = tiles[at][half * LEFT : (half + 1) * LEFT]
                else:
                    out[c, side, pl.ds(part * 4 + z, TILE, stride=16), :] = tiles[at]
            return carry

        lax.fori_loop(0, n_py // 8, side_step, 0)

    loads[2].wait()
    loads[3].wait()
    pack(0)
    pl.semaphore_wait(barrier, n_pz - 1 + n_py - 1)
    send_opposite(0)
    send(0)
    loads[5].wait()
    pack(1)
    send_opposite(1)
    forward(0)
    send(1)
    loads[6].wait()
    pack(2)
    send_opposite(2)
    send_opposite(3)
    loads[4].wait()
    local = lax.broadcasted_iota(jnp.int32, (place.shape[0], total_slots), 0)
    place[...] = jnp.where(local == arrival_here[...], 1.0, 0.0).astype(BF16)
    loads[7].wait()
    forward(1)
    receive(0)
    send(2)
    transform(0, 0)
    transform(0, 1)
    spread(0)
    receive(1)
    forward(2)
    forward(3)
    transform(1, 0)
    transform(1, 1)
    spread(1)
    send(3)
    receive(2)
    transform(2, 0)
    spread(2)
    gather(0)
    for part in range(3):
        put_in_order(0, part)
    receive(3)
    transform(2, 1)
    spread(3)
    gather(1)
    for part in range(3):
        put_in_order(1, part)
    gather(2)
    put_in_order(2, 0)
    gather(3)
    put_in_order(2, 1)
    put_in_order(2, 2)
    for wave in range(len(WAVES)):
        wait_for(block(outgoing, wave, pl.ds(0, n_pz - 1)), send_sem.at[wave])
        wait_for(block(relayed, wave, pl.ds(0, X_RING)), forward_sem.at[wave])
        wait_for(piece(coeffs, wave, pl.ds(0, n_py - 1)), spread_sem.at[wave])


def transfer(n_py, n_pz, nodal, counts, send_slots, arrival_slots):
    capacity, values = nodal.shape[1:]
    total_slots = n_pz * SLOTS
    elements = total_slots // 2 // BLOCKS
    fourier = jnp.asarray(fourier_table(n_py, elements))
    plane = jnp.asarray(plane_table())
    remote = pl.BlockSpec(memory_space=pltpu.HBM)
    here = functools.partial(pltpu.with_memory_space_constraint, memory_space=pltpu.HBM)
    return pl.pallas_call(
        functools.partial(transfer_kernel, n_py, n_pz),
        out_shape=jax.ShapeDtypeStruct((COMPONENTS, n_py // 8, USED * 16, 128), F32),
        in_specs=[remote] * 6,
        out_specs=pl.BlockSpec(memory_space=pltpu.VMEM),
        scratch_shapes=[
            pltpu.VMEM((COMPONENTS, capacity, values), BF16),
            pltpu.VMEM(counts.shape, jnp.int32),
            pltpu.VMEM(send_slots.shape, jnp.int32),
            pltpu.VMEM(arrival_slots.shape, jnp.int32),
            pltpu.VMEM(fourier.shape, BF16),
            pltpu.VMEM(plane.shape, BF16),
            pltpu.VMEM((total_slots, capacity), BF16),
            pltpu.VMEM((total_slots // 2, total_slots), BF16),
            pltpu.VMEM((COMPONENTS, n_pz, 2, SLOTS, WIDTH), BF16),
            pltpu.VMEM((COMPONENTS, X_RING, 2, SLOTS, WIDTH), BF16),
            pltpu.VMEM((COMPONENTS, n_pz, 2, SLOTS, WIDTH), BF16),
            pltpu.VMEM((NODE * elements, 128), BF16),
            pltpu.VMEM((n_py * TILE, 128), F32),
            pltpu.VMEM((COMPONENTS, n_py, 3, TILE, 128), BF16),
            pltpu.VMEM((COMPONENTS, n_py, 3, TILE, 128), BF16),
            pltpu.SemaphoreType.DMA((8,)),
            *[pltpu.SemaphoreType.DMA((len(WAVES),)) for _ in range(6)],
        ],
        compiler_params=pltpu.CompilerParams(
            collective_id=0, has_side_effects=True, vmem_limit_bytes=40 * 1024 * 1024
        ),
    )(
        here(nodal), counts, here(send_slots), here(arrival_slots), here(fourier), here(plane)
    )


def write_kernel(spectra, out, sem):
    copies = [
        pltpu.make_async_copy(
            spectra.at[c, side], out.at[c, :, pl.ds(side * 128, 128)], sem.at[c, side]
        )
        for c in range(COMPONENTS)
        for side in range(spectra.shape[1])
    ]
    for copy in copies:
        copy.start()
    for copy in copies:
        copy.wait()


def write(spectra):
    sides, rows = spectra.shape[1:3]
    anywhere = pl.BlockSpec(memory_space=pl.ANY)
    return pl.pallas_call(
        write_kernel,
        out_shape=jax.ShapeDtypeStruct((COMPONENTS, rows, sides * 128), F32),
        in_specs=[anywhere],
        out_specs=anywhere,
        scratch_shapes=[pltpu.SemaphoreType.DMA((COMPONENTS, sides))],
        compiler_params=pltpu.CompilerParams(vmem_limit_bytes=40 * 1024 * 1024),
    )(spectra)


def solution(mesh):
    n_py, n_pz = mesh.shape["py"], mesh.shape["pz"]

    def on_device(nodal, element_counts, send_slots, arrival_slots):
        turned = nodal[0].transpose(1, 0, 2)
        spectra = transfer(n_py, n_pz, turned, element_counts, send_slots, arrival_slots)
        return write(spectra).reshape(COMPONENTS, 2, MODES, 16, -1)

    placed = (P("py", "pz", None, None), P("py", "pz"), P("py", "pz"), P("py", "pz"))
    return jax.shard_map(
        on_device,
        mesh=mesh,
        in_specs=placed,
        out_specs=P(None, None, "py", "pz", None),
        check_vma=False,
    )
```

```python
import functools
import math

import jax
import jax.numpy as jnp
import ml_dtypes
import numpy as np
from jax import lax
from jax.experimental import pallas as pl
from jax.experimental.pallas import tpu as pltpu
from jax.sharding import PartitionSpec as P

NODE = 8
YE = 2
LZ = 2
BLOCKS = YE * LZ
COMPONENTS = 3
SLOTS = 16
X_RING = 4
MODES = 10
USED = 2 * MODES
TILE = 16
LEFT = USED - TILE
GROUP = 8
WAVES = ((0, 0, 2, 0, 256), (1, 0, 2, 0, 256), (2, 0, 1, 0, 256), (2, 1, 1, 0, 128), (2, 1, 1, 128, 128))
PARTS = ((0, 0, 3), (1, 0, 3), (2, 0, 2), (2, 2, 1), (2, 3, 1))
LAST = COMPONENTS - 1
WIDTH = NODE**3 // 2
BF16 = jnp.bfloat16
F32 = jnp.float32
MESH = pl.DeviceIdType.MESH


def lobatto_points(number):
    degree = number - 1
    points = np.cos(np.pi * np.arange(number) / degree)
    for sweeps in range(60):
        older_poly = np.ones(number)
        newer_poly = points.copy()
        for degree_now in range(2, degree + 1):
            older_poly, newer_poly = (
                newer_poly,
                ((2 * degree_now - 1) * points * newer_poly - (degree_now - 1) * older_poly)
                / degree_now,
            )
        points = points - (points * newer_poly - older_poly) / (number * newer_poly)
    return np.sort(points)


def vandermonde(number):
    gauss_points = lobatto_points(number)
    uniform = -1.0 + (2.0 * np.arange(number) + 1.0) / number
    columns_list = []
    for column in range(number):
        same = np.arange(number) == column
        numer = np.where(same[None, :], 1.0, uniform[:, None] - gauss_points[None, :])
        denom = np.where(same, 1.0, gauss_points[column] - gauss_points)
        columns_list.append(np.prod(numer / denom[None, :], axis=1))
    return np.stack(columns_list, axis=1)


def fourier_table(bands, elements):
    length = elements * NODE
    wavenumber = np.arange(bands * MODES)[:, None]
    angles = (wavenumber * np.arange(length)[None, :] % length) * (2.0 * np.pi / length)
    dft = np.stack([np.cos(angles), -np.sin(angles)]) / math.sqrt(length)
    dft = dft.reshape(2, bands, MODES, elements, NODE)
    nodes = np.einsum("tikeh,hn->itkne", dft, vandermonde(NODE))
    nodes = nodes.reshape(bands, USED, NODE, elements)
    table = np.zeros((2, bands, TILE, NODE, elements))
    table[0] = nodes[:, :TILE]
    table[1, :, :LEFT] = nodes[:, TILE:]
    return table.reshape(2, bands * TILE, NODE * elements).astype(ml_dtypes.bfloat16)


def plane_table():
    lagrange = vandermonde(NODE)
    table = np.einsum("fu,gv,hw->uvhwfg", lagrange, lagrange, np.eye(NODE))
    halves = table.reshape(NODE**3, NODE, 2, NODE // 2, NODE).transpose(2, 0, 1, 3, 4)
    quarters = halves[1].reshape(NODE**3, NODE, 2, NODE // 4, NODE).transpose(0, 2, 1, 3, 4)
    tables = [halves[0], halves[1], quarters]
    tables = [table.reshape(NODE**3, NODE**3 // 2) for table in tables]
    return np.stack(tables).astype(ml_dtypes.bfloat16)


def exchange(tiles, index_bit, lane_bit, width):
    lane = lax.broadcasted_iota(jnp.int32, tiles[0].shape, 1)
    shift = lane_bit * width
    low = lane % (2 * shift) < shift
    turned = list(tiles)
    for at in range(len(tiles)):
        if at & index_bit == 0:
            first, second = tiles[at], tiles[at + index_bit]
            turned[at] = jnp.where(low, first, pltpu.roll(second, shift, 1))
            turned[at + index_bit] = jnp.where(low, pltpu.roll(first, 128 - shift, 1), second)
    return turned


def transfer_kernel(
    n_py, n_pz, nodal, counts, send_slots, arrival_slots, fourier, plane, out,
    nodes, counts_here, send_here, arrival_here, fourier_here, plane_here, pick, place,
    outgoing, relayed, arrived, stacked, leftover, coeffs, received,
    load_sem, send_sem, relay_sem, forward_sem, arrive_sem, spread_sem, receive_sem,
):
    me_y = lax.axis_index("py")
    me_z = lax.axis_index("pz")
    z_ring = n_pz // X_RING
    my_plane, my_column = me_z // X_RING, me_z % X_RING
    capacity = nodes.shape[1]
    elements = place.shape[0] // BLOCKS
    total_slots = n_pz * SLOTS

    barrier = pltpu.get_barrier_semaphore()

    def greet_z(step, carry):
        pl.semaphore_signal(
            barrier, inc=1, device_id={"pz": (me_z + step) % n_pz}, device_id_type=MESH
        )
        return carry

    def greet_y(step, carry):
        pl.semaphore_signal(
            barrier, inc=1, device_id={"py": (me_y + step) % n_py}, device_id_type=MESH
        )
        return carry

    pairs = [
        (send_slots, send_here),
        (counts, counts_here),
        (nodal.at[0], nodes.at[0]),
        (plane, plane_here),
        (arrival_slots, arrival_here),
        (nodal.at[1], nodes.at[1]),
        (nodal.at[2], nodes.at[2]),
        (fourier, fourier_here),
    ]
    loads = [
        pltpu.make_async_copy(source, here, load_sem.at[at])
        for at, (source, here) in enumerate(pairs)
    ]
    for load in loads:
        load.start()
    lax.fori_loop(1, n_pz, greet_z, 0)
    lax.fori_loop(1, n_py, greet_y, 0)

    loads[0].wait()
    loads[1].wait()
    column = lax.broadcasted_iota(jnp.int32, (1, capacity), 1)
    target = jnp.where(column < counts_here[...], send_here[...], -1)
    row = lax.broadcasted_iota(jnp.int32, (total_slots, capacity), 0)
    pick[...] = jnp.where(row == target, 1.0, 0.0).astype(BF16)

    def pack(c):
        for half in range(2):
            table = plane_here[2 if c == LAST and half == 1 else half]
            turned = jnp.dot(nodes[c], table, preferred_element_type=F32).astype(BF16)
            packed = jnp.dot(pick[...], turned, preferred_element_type=F32).astype(BF16)
            outgoing[c, :, half] = packed.reshape(n_pz, SLOTS, WIDTH)

    def peer_at(plane_step, column_step):
        peer_plane = (my_plane + plane_step + z_ring) % z_ring
        return peer_plane * X_RING + (my_column + column_step + X_RING) % X_RING

    def block(ref, wave, device):
        c, first, number, lane, lanes = WAVES[wave]
        return ref.at[c, device, pl.ds(first, number), :, pl.ds(lane, lanes)]

    def piece(ref, wave, device):
        c, first, number = PARTS[wave]
        return ref.at[c, device, pl.ds(first, number)]

    def wait_for(part, sem):
        pltpu.make_async_copy(part, part, sem).wait()

    def send_to(wave, plane_step, column_step):
        peer = peer_at(plane_step, column_step)
        pltpu.make_async_remote_copy(
            src_ref=block(outgoing, wave, peer),
            dst_ref=block(arrived, wave, me_z),
            send_sem=send_sem.at[wave],
            recv_sem=arrive_sem.at[wave],
            device_id={"pz": peer},
            device_id_type=MESH,
        ).start()

    quarter = z_ring // 4

    def send_opposite(wave):
        def opposite(step, carry):
            way = (1 - step % 2 * 2) * quarter
            pltpu.make_async_remote_copy(
                src_ref=block(outgoing, wave, peer_at(2 * quarter, step)),
                dst_ref=block(relayed, wave, step),
                send_sem=send_sem.at[wave],
                recv_sem=relay_sem.at[wave],
                device_id={"pz": peer_at(way, step)},
                device_id_type=MESH,
            ).start()
            return carry

        lax.fori_loop(0, X_RING, opposite, 0)

    def send(wave):
        def far(step, carry):
            side = 1 - (step + me_y) % 2 * 2
            pair = step // 2
            send_to(wave, side * (pair % (z_ring // 2 - 1) + 1), side * (pair % X_RING))
            return carry

        def near(step, carry):
            send_to(wave, 0, step)
            return carry

        lax.fori_loop(1, X_RING, near, 0)
        lax.fori_loop(0, (z_ring - 2) * X_RING, far, 0)
        c, first, number, lane, lanes = WAVES[wave]
        here = pl.ds(lane, lanes)
        for half in range(first, first + number):
            arrived[c, me_z, half, :, here] = outgoing[c, me_z, half, :, here]

    def forward(wave):
        wait_for(block(relayed, wave, pl.ds(0, X_RING)), relay_sem.at[wave])

        def onward(step, carry):
            way = (1 - step % 2 * 2) * quarter
            pltpu.make_async_remote_copy(
                src_ref=block(relayed, wave, step),
                dst_ref=block(arrived, wave, peer_at(-way, -step)),
                send_sem=forward_sem.at[wave],
                recv_sem=arrive_sem.at[wave],
                device_id={"pz": peer_at(way, 0)},
                device_id_type=MESH,
            ).start()
            return carry

        lax.fori_loop(0, X_RING, onward, 0)

    def receive(wave):
        wait_for(block(arrived, wave, pl.ds(0, n_pz - 1)), arrive_sem.at[wave])

    rows = GROUP * TILE
    groups = n_py // GROUP

    def transform(c, half):
        slots = arrived[c, :, half].reshape(total_slots, WIDTH)
        placed = jnp.dot(place[...], slots, preferred_element_type=F32)
        for quad in range(2):
            tiles = [
                placed[at * elements : (at + 1) * elements, quad * 128 : (quad + 1) * 128]
                for at in range(BLOCKS)
            ]
            tiles = exchange(exchange(tiles, 1, 1, 32), 2, 2, 32)
            for at, tile in enumerate(tiles):
                stacked[pl.ds((quad * 4 + at) * elements, elements), :] = tile.astype(BF16)

        def group_step(step, carry):
            here = pl.ds(pl.multiple_of(step * rows, rows), rows)
            members = pl.ds(step * GROUP, GROUP)
            result = jnp.dot(fourier_here[0, here], stacked[...], preferred_element_type=F32)
            coeffs[c, members, half] = result.astype(BF16).reshape(GROUP, TILE, 128)
            rest = jnp.dot(fourier_here[1, here], stacked[...], preferred_element_type=F32)
            if c == LAST:
                coeffs[c, members, 1] = rest.astype(BF16).reshape(GROUP, TILE, 128)
            elif half == 0:
                leftover[here] = rest
            else:
                both = leftover[here] + pltpu.roll(rest, LEFT, 0)
                coeffs[c, members, 2] = both.astype(BF16).reshape(GROUP, TILE, 128)
            return carry

        lax.fori_loop(0, groups, group_step, 0)

    def transform_quarter(quarter_at):
        slots = arrived[LAST, :, 1, :, pl.ds(quarter_at * 128, 128)].reshape(total_slots, 128)
        placed = jnp.dot(place[...], slots, preferred_element_type=F32)
        tiles = [placed[at * elements : (at + 1) * elements] for at in range(BLOCKS)]
        tiles = exchange(exchange(tiles, 1, 1, 16), 2, 2, 16)
        for at, tile in enumerate(tiles):
            stacked[pl.ds(at * elements, elements), :] = tile.astype(BF16)
            stacked[pl.ds((4 + at) * elements, elements), :] = pltpu.roll(tile, 64, 1).astype(BF16)

        def group_step(step, carry):
            here = pl.ds(pl.multiple_of(step * rows, rows), rows)
            result = jnp.dot(fourier_here[0, here], stacked[...], preferred_element_type=F32)
            rest = jnp.dot(fourier_here[1, here], stacked[...], preferred_element_type=F32)
            lane = lax.broadcasted_iota(jnp.int32, result.shape, 1)
            both = jnp.where(lane < 64, result, pltpu.roll(rest, 64, 1))
            coeffs[LAST, pl.ds(step * GROUP, GROUP), 2 + quarter_at] = both.astype(BF16).reshape(
                GROUP, TILE, 128
            )
            return carry

        lax.fori_loop(0, groups, group_step, 0)

    def spread(wave):
        c, first, number = PARTS[wave]
        for part in range(first, first + number):
            received[c, me_y, part] = coeffs[c, me_y, part]

        def spread_to(step, carry):
            peer = (me_y + (step + 1) // 2 * (1 - step % 2 * 2) + n_py) % n_py
            pltpu.make_async_remote_copy(
                src_ref=piece(coeffs, wave, peer),
                dst_ref=piece(received, wave, me_y),
                send_sem=spread_sem.at[wave],
                recv_sem=receive_sem.at[wave],
                device_id={"py": peer},
                device_id_type=MESH,
            ).start()
            return carry

        lax.fori_loop(1, n_py, spread_to, 0)

    def gather(wave):
        wait_for(piece(received, wave, pl.ds(0, n_py - 1)), receive_sem.at[wave])

    def put_in_order(c, part):
        rest = part == (1 if c == LAST else 2)

        def side_step(side, carry):
            tiles = [received[c, side * 8 + band, part].astype(F32) for band in range(8)]
            if rest:
                tiles = [tile[: 2 * LEFT] for tile in tiles]
            for index_bit, lane_bit in ((4, 8), (2, 4), (1, 2), (2, 1)):
                tiles = exchange(tiles, index_bit, lane_bit, 8)
            for at in range(8):
                z = at // 4 * 8 + at % 2 * 2 + at // 2 % 2
                if rest:
                    for half in range(1 if c == LAST else 2):
                        here = pl.ds(TILE * 16 + half * 4 + z, LEFT, stride=16)
                        out[c, side, here, :] = tiles[at][half * LEFT : (half + 1) * LEFT]
                else:
                    out[c, side, pl.ds(part * 4 + z, TILE, stride=16), :] = tiles[at]
            return carry

        lax.fori_loop(0, n_py // 8, side_step, 0)

    def put_quarter_in_order(quarter_at):
        def side_step(side, carry):
            tiles = [
                received[LAST, side * 8 + band, 2 + quarter_at].astype(F32) for band in range(8)
            ]
            for index_bit, lane_bit in ((4, 8), (2, 4), (1, 2), (1, 1)):
                tiles = exchange(tiles, index_bit, lane_bit, 8)
            for at in range(8):
                z = 4 + quarter_at * 2 + at // 2 % 2 * 8 + at % 2
                if at < 4:
                    out[LAST, side, pl.ds(z, TILE, stride=16), :] = tiles[at]
                else:
                    here = pl.ds(TILE * 16 + z, LEFT, stride=16)
                    out[LAST, side, here, :] = tiles[at][:LEFT]
            return carry

        lax.fori_loop(0, n_py // 8, side_step, 0)

    loads[2].wait()
    loads[3].wait()
    pack(0)
    pl.semaphore_wait(barrier, n_pz - 1 + n_py - 1)
    send_opposite(0)
    send(0)
    loads[5].wait()
    pack(1)
    send_opposite(1)
    forward(0)
    send(1)
    loads[6].wait()
    pack(2)
    send_opposite(2)
    send_opposite(3)
    send_opposite(4)
    loads[4].wait()
    local = lax.broadcasted_iota(jnp.int32, (place.shape[0], total_slots), 0)
    place[...] = jnp.where(local == arrival_here[...], 1.0, 0.0).astype(BF16)
    loads[7].wait()
    forward(1)
    receive(0)
    send(2)
    transform(0, 0)
    transform(0, 1)
    spread(0)
    receive(1)
    forward(2)
    forward(3)
    forward(4)
    transform(1, 0)
    transform(1, 1)
    spread(1)
    send(3)
    send(4)
    receive(2)
    transform(2, 0)
    spread(2)
    gather(0)
    for part in range(3):
        put_in_order(0, part)
    receive(3)
    transform_quarter(0)
    spread(3)
    receive(4)
    transform_quarter(1)
    spread(4)
    gather(1)
    for part in range(3):
        put_in_order(1, part)
    gather(2)
    put_in_order(2, 0)
    put_in_order(2, 1)
    gather(3)
    put_quarter_in_order(0)
    gather(4)
    put_quarter_in_order(1)
    for wave in range(len(WAVES)):
        wait_for(block(outgoing, wave, pl.ds(0, n_pz - 1)), send_sem.at[wave])
        wait_for(block(relayed, wave, pl.ds(0, X_RING)), forward_sem.at[wave])
        wait_for(piece(coeffs, wave, pl.ds(0, n_py - 1)), spread_sem.at[wave])


def transfer(n_py, n_pz, nodal, counts, send_slots, arrival_slots):
    capacity, values = nodal.shape[1:]
    total_slots = n_pz * SLOTS
    elements = total_slots // 2 // BLOCKS
    fourier = jnp.asarray(fourier_table(n_py, elements))
    plane = jnp.asarray(plane_table())
    remote = pl.BlockSpec(memory_space=pltpu.HBM)
    here = functools.partial(pltpu.with_memory_space_constraint, memory_space=pltpu.HBM)
    return pl.pallas_call(
        functools.partial(transfer_kernel, n_py, n_pz),
        out_shape=jax.ShapeDtypeStruct((COMPONENTS, n_py // 8, USED * 16, 128), F32),
        in_specs=[remote] * 6,
        out_specs=pl.BlockSpec(memory_space=pltpu.VMEM),
        scratch_shapes=[
            pltpu.VMEM((COMPONENTS, capacity, values), BF16),
            pltpu.VMEM(counts.shape, jnp.int32),
            pltpu.VMEM(send_slots.shape, jnp.int32),
            pltpu.VMEM(arrival_slots.shape, jnp.int32),
            pltpu.VMEM(fourier.shape, BF16),
            pltpu.VMEM(plane.shape, BF16),
            pltpu.VMEM((total_slots, capacity), BF16),
            pltpu.VMEM((total_slots // 2, total_slots), BF16),
            pltpu.VMEM((COMPONENTS, n_pz, 2, SLOTS, WIDTH), BF16),
            pltpu.VMEM((COMPONENTS, X_RING, 2, SLOTS, WIDTH), BF16),
            pltpu.VMEM((COMPONENTS, n_pz, 2, SLOTS, WIDTH), BF16),
            pltpu.VMEM((NODE * elements, 128), BF16),
            pltpu.VMEM((n_py * TILE, 128), F32),
            pltpu.VMEM((COMPONENTS, n_py, 4, TILE, 128), BF16),
            pltpu.VMEM((COMPONENTS, n_py, 4, TILE, 128), BF16),
            pltpu.SemaphoreType.DMA((8,)),
            *[pltpu.SemaphoreType.DMA((len(WAVES),)) for _ in range(6)],
        ],
        compiler_params=pltpu.CompilerParams(
            collective_id=0, has_side_effects=True, vmem_limit_bytes=40 * 1024 * 1024
        ),
    )(
        here(nodal), counts, here(send_slots), here(arrival_slots), here(fourier), here(plane)
    )


def write_kernel(spectra, out, sem):
    copies = [
        pltpu.make_async_copy(
            spectra.at[c, side], out.at[c, :, pl.ds(side * 128, 128)], sem.at[c, side]
        )
        for c in range(COMPONENTS)
        for side in range(spectra.shape[1])
    ]
    for copy in copies:
        copy.start()
    for copy in copies:
        copy.wait()


def write(spectra):
    sides, rows = spectra.shape[1:3]
    anywhere = pl.BlockSpec(memory_space=pl.ANY)
    return pl.pallas_call(
        write_kernel,
        out_shape=jax.ShapeDtypeStruct((COMPONENTS, rows, sides * 128), F32),
        in_specs=[anywhere],
        out_specs=anywhere,
        scratch_shapes=[pltpu.SemaphoreType.DMA((COMPONENTS, sides))],
        compiler_params=pltpu.CompilerParams(vmem_limit_bytes=40 * 1024 * 1024),
    )(spectra)


def solution(mesh):
    n_py, n_pz = mesh.shape["py"], mesh.shape["pz"]

    def on_device(nodal, element_counts, send_slots, arrival_slots):
        turned = nodal[0].transpose(1, 0, 2)
        spectra = transfer(n_py, n_pz, turned, element_counts, send_slots, arrival_slots)
        return write(spectra).reshape(COMPONENTS, 2, MODES, 16, -1)

    placed = (P("py", "pz", None, None), P("py", "pz"), P("py", "pz"), P("py", "pz"))
    return jax.shard_map(
        on_device,
        mesh=mesh,
        in_specs=placed,
        out_specs=P(None, None, "py", "pz", None),
        check_vma=False,
    )
```

```python
import functools
import math

import jax
import jax.numpy as jnp
import ml_dtypes
import numpy as np
from jax import lax
from jax.experimental import pallas as pl
from jax.experimental.pallas import tpu as pltpu
from jax.sharding import PartitionSpec as P

NODE = 8
YE = 2
LZ = 2
BLOCKS = YE * LZ
COMPONENTS = 3
SLOTS = 16
X_RING = 4
MODES = 10
USED = 2 * MODES
TILE = 16
LEFT = USED - TILE
WAVES = ((0, 0, 2), (1, 0, 2), (2, 0, 1), (2, 1, 1))
PARTS = ((0, 0, 3), (1, 0, 3), (2, 0, 1), (2, 1, 2))
WIDTH = NODE**3 // 2
BF16 = jnp.bfloat16
F32 = jnp.float32
MESH = pl.DeviceIdType.MESH


def lobatto_points(number):
    degree = number - 1
    points = np.cos(np.pi * np.arange(number) / degree)
    for sweeps in range(60):
        older_poly = np.ones(number)
        newer_poly = points.copy()
        for degree_now in range(2, degree + 1):
            older_poly, newer_poly = (
                newer_poly,
                ((2 * degree_now - 1) * points * newer_poly - (degree_now - 1) * older_poly)
                / degree_now,
            )
        points = points - (points * newer_poly - older_poly) / (number * newer_poly)
    return np.sort(points)


def vandermonde(number):
    gauss_points = lobatto_points(number)
    uniform = -1.0 + (2.0 * np.arange(number) + 1.0) / number
    columns_list = []
    for column in range(number):
        same = np.arange(number) == column
        numer = np.where(same[None, :], 1.0, uniform[:, None] - gauss_points[None, :])
        denom = np.where(same, 1.0, gauss_points[column] - gauss_points)
        columns_list.append(np.prod(numer / denom[None, :], axis=1))
    return np.stack(columns_list, axis=1)


def fourier_table(bands, elements):
    length = elements * NODE
    wavenumber = np.arange(bands * MODES)[:, None]
    angles = (wavenumber * np.arange(length)[None, :] % length) * (2.0 * np.pi / length)
    dft = np.stack([np.cos(angles), -np.sin(angles)]) / math.sqrt(length)
    dft = dft.reshape(2, bands, MODES, elements, NODE)
    nodes = np.einsum("tikeh,hn->itkne", dft, vandermonde(NODE))
    nodes = nodes.reshape(bands, USED, NODE, elements)
    table = np.zeros((2, bands, TILE, NODE, elements))
    table[0] = nodes[:, :TILE]
    table[1, :, :LEFT] = nodes[:, TILE:]
    return table.reshape(2 * bands * TILE, NODE * elements).astype(ml_dtypes.bfloat16)


def plane_table():
    lagrange = vandermonde(NODE)
    table = np.einsum("fu,gv,hw->uvhwfg", lagrange, lagrange, np.eye(NODE))
    table = table.reshape(NODE**3, NODE, 2, NODE // 2, NODE).transpose(2, 0, 1, 3, 4)
    return table.reshape(2, NODE**3, NODE**3 // 2).astype(ml_dtypes.bfloat16)


def exchange(tiles, index_bit, lane_bit, width):
    lane = lax.broadcasted_iota(jnp.int32, tiles[0].shape, 1)
    shift = lane_bit * width
    low = lane % (2 * shift) < shift
    turned = list(tiles)
    for at in range(len(tiles)):
        if at & index_bit == 0:
            first, second = tiles[at], tiles[at + index_bit]
            turned[at] = jnp.where(low, first, pltpu.roll(second, shift, 1))
            turned[at + index_bit] = jnp.where(low, pltpu.roll(first, 128 - shift, 1), second)
    return turned


def transfer_kernel(
    n_py, n_pz, nodal, counts, send_slots, arrival_slots, fourier, plane, out,
    nodes, counts_here, send_here, arrival_here, fourier_here, plane_here, pick, place,
    outgoing, relayed, arrived, stacked, leftover, coeffs, received,
    load_sem, send_sem, relay_sem, forward_sem, arrive_sem, spread_sem, receive_sem,
):
    me_y = lax.axis_index("py")
    me_z = lax.axis_index("pz")
    z_ring = n_pz // X_RING
    my_plane, my_column = me_z // X_RING, me_z % X_RING
    capacity = nodes.shape[1]
    elements = place.shape[0] // BLOCKS
    total_slots = n_pz * SLOTS

    barrier = pltpu.get_barrier_semaphore()

    def greet_z(step, carry):
        pl.semaphore_signal(
            barrier, inc=1, device_id={"pz": (me_z + step) % n_pz}, device_id_type=MESH
        )
        return carry

    def greet_y(step, carry):
        pl.semaphore_signal(
            barrier, inc=1, device_id={"py": (me_y + step) % n_py}, device_id_type=MESH
        )
        return carry

    pairs = [
        (send_slots, send_here),
        (counts, counts_here),
        (nodal.at[0], nodes.at[0]),
        (plane, plane_here),
        (arrival_slots, arrival_here),
        (nodal.at[1], nodes.at[1]),
        (nodal.at[2], nodes.at[2]),
        (fourier, fourier_here),
    ]
    loads = [
        pltpu.make_async_copy(source, here, load_sem.at[at])
        for at, (source, here) in enumerate(pairs)
    ]
    for load in loads:
        load.start()
    lax.fori_loop(1, n_pz, greet_z, 0)
    lax.fori_loop(1, n_py, greet_y, 0)

    loads[0].wait()
    loads[1].wait()
    column = lax.broadcasted_iota(jnp.int32, (1, capacity), 1)
    target = jnp.where(column < counts_here[...], send_here[...], -1)
    row = lax.broadcasted_iota(jnp.int32, (total_slots, capacity), 0)
    pick[...] = jnp.where(row == target, 1.0, 0.0).astype(BF16)

    def pack(c):
        for half in range(2):
            turned = jnp.dot(nodes[c], plane_here[half], preferred_element_type=F32).astype(BF16)
            packed = jnp.dot(pick[...], turned, preferred_element_type=F32).astype(BF16)
            outgoing[c, :, half] = packed.reshape(n_pz, SLOTS, WIDTH)

    def peer_at(plane_step, column_step):
        peer_plane = (my_plane + plane_step + z_ring) % z_ring
        return peer_plane * X_RING + (my_column + column_step + X_RING) % X_RING

    def block(ref, wave, device):
        c, first, number = WAVES[wave]
        return ref.at[c, device, pl.ds(first, number)]

    def piece(ref, wave, device):
        c, first, number = PARTS[wave]
        return ref.at[c, device, pl.ds(first, number)]

    def wait_for(part, sem):
        pltpu.make_async_copy(part, part, sem).wait()

    def send_to(wave, plane_step, column_step):
        peer = peer_at(plane_step, column_step)
        pltpu.make_async_remote_copy(
            src_ref=block(outgoing, wave, peer),
            dst_ref=block(arrived, wave, me_z),
            send_sem=send_sem.at[wave],
            recv_sem=arrive_sem.at[wave],
            device_id={"pz": peer},
            device_id_type=MESH,
        ).start()

    quarter = z_ring // 4
    first_side = 1 - me_y % 2 * 2

    def send_opposite(wave):
        for step in range(X_RING):
            way = (1 - step % 2 * 2) * quarter
            pltpu.make_async_remote_copy(
                src_ref=block(outgoing, wave, peer_at(2 * quarter, step)),
                dst_ref=block(relayed, wave, step),
                send_sem=send_sem.at[wave],
                recv_sem=relay_sem.at[wave],
                device_id={"pz": peer_at(way, step)},
                device_id_type=MESH,
            ).start()

    pairs_far = [(p % (z_ring // 2 - 1) + 1, p % X_RING) for p in range((z_ring // 2 - 1) * X_RING)]

    def send_far(wave, chosen):
        for distance, column in chosen:
            for side in (first_side, -first_side):
                send_to(wave, side * distance, side * column)

    def send_near(wave):
        for column in range(1, X_RING):
            send_to(wave, 0, column)
        c, first, number = WAVES[wave]
        for half in range(first, first + number):
            arrived[c, me_z, half] = outgoing[c, me_z, half]

    def send(wave):
        send_near(wave)
        send_far(wave, pairs_far)

    def forward(wave):
        wait_for(block(relayed, wave, pl.ds(0, X_RING)), relay_sem.at[wave])

        for step in range(X_RING):
            way = (1 - step % 2 * 2) * quarter
            pltpu.make_async_remote_copy(
                src_ref=block(relayed, wave, step),
                dst_ref=block(arrived, wave, peer_at(-way, -step)),
                send_sem=forward_sem.at[wave],
                recv_sem=arrive_sem.at[wave],
                device_id={"pz": peer_at(way, 0)},
                device_id_type=MESH,
            ).start()

    def receive(wave):
        wait_for(block(arrived, wave, pl.ds(0, n_pz - 1)), arrive_sem.at[wave])

    def transform(c, half):
        slots = arrived[c, :, half].reshape(total_slots, WIDTH)
        placed = jnp.dot(place[...], slots, preferred_element_type=F32)
        for quad in range(2):
            tiles = [
                placed[at * elements : (at + 1) * elements, quad * 128 : (quad + 1) * 128]
                for at in range(BLOCKS)
            ]
            tiles = exchange(exchange(tiles, 1, 1, 32), 2, 2, 32)
            for at, tile in enumerate(tiles):
                stacked[pl.ds((quad * 4 + at) * elements, elements), :] = tile.astype(BF16)

        result = jnp.dot(fourier_here[...], stacked[...], preferred_element_type=F32)
        main, rest = result[: n_py * TILE], result[n_py * TILE :]
        coeffs[c, :, half] = main.astype(BF16).reshape(n_py, TILE, 128)
        if half == 0:
            leftover[...] = rest
        else:
            both = leftover[...] + pltpu.roll(rest, LEFT, 0)
            coeffs[c, :, 2] = both.astype(BF16).reshape(n_py, TILE, 128)

    def spread(wave):
        c, first, number = PARTS[wave]
        for part in range(first, first + number):
            received[c, me_y, part] = coeffs[c, me_y, part]

        for step in range(1, n_py):
            peer = (me_y + (step + 1) // 2 * (1 - step % 2 * 2) + n_py) % n_py
            pltpu.make_async_remote_copy(
                src_ref=piece(coeffs, wave, peer),
                dst_ref=piece(received, wave, me_y),
                send_sem=spread_sem.at[wave],
                recv_sem=receive_sem.at[wave],
                device_id={"py": peer},
                device_id_type=MESH,
            ).start()

    def gather(wave):
        wait_for(piece(received, wave, pl.ds(0, n_py - 1)), receive_sem.at[wave])

    def put_in_order(c, part):
        def side_step(side, carry):
            tiles = [received[c, side * 8 + band, part].astype(F32) for band in range(8)]
            if part == 2:
                tiles = [tile[: 2 * LEFT] for tile in tiles]
            for index_bit, lane_bit in ((4, 8), (2, 4), (1, 2), (2, 1)):
                tiles = exchange(tiles, index_bit, lane_bit, 8)
            for at in range(8):
                z = at // 4 * 8 + at % 2 * 2 + at // 2 % 2
                if part == 2:
                    for half in range(2):
                        here = pl.ds(TILE * 16 + half * 4 + z, LEFT, stride=16)
                        out[c, side, here, :] = tiles[at][half * LEFT : (half + 1) * LEFT]
                else:
                    out[c, side, pl.ds(part * 4 + z, TILE, stride=16), :] = tiles[at]
            return carry

        lax.fori_loop(0, n_py // 8, side_step, 0)

    loads[2].wait()
    loads[3].wait()
    pack(0)
    pl.semaphore_wait(barrier, n_pz - 1 + n_py - 1)
    send_opposite(0)
    send(0)
    loads[5].wait()
    pack(1)
    send_opposite(1)
    forward(0)
    send(1)
    loads[6].wait()
    pack(2)
    send_opposite(2)
    send_opposite(3)
    loads[4].wait()
    local = lax.broadcasted_iota(jnp.int32, (place.shape[0], total_slots), 0)
    place[...] = jnp.where(local == arrival_here[...], 1.0, 0.0).astype(BF16)
    loads[7].wait()
    forward(1)
    receive(0)
    send(2)
    transform(0, 0)
    transform(0, 1)
    spread(0)
    receive(1)
    forward(2)
    forward(3)
    transform(1, 0)
    send_near(3)
    send_far(3, pairs_far[: len(pairs_far) // 2])
    transform(1, 1)
    spread(1)
    send_far(3, pairs_far[len(pairs_far) // 2 :])
    receive(2)
    transform(2, 0)
    spread(2)
    gather(0)
    for part in range(3):
        put_in_order(0, part)
    receive(3)
    transform(2, 1)
    spread(3)
    gather(1)
    for part in range(3):
        put_in_order(1, part)
    gather(2)
    put_in_order(2, 0)
    gather(3)
    put_in_order(2, 1)
    put_in_order(2, 2)
    for wave in range(len(WAVES)):
        wait_for(block(outgoing, wave, pl.ds(0, n_pz - 1)), send_sem.at[wave])
        wait_for(block(relayed, wave, pl.ds(0, X_RING)), forward_sem.at[wave])
        wait_for(piece(coeffs, wave, pl.ds(0, n_py - 1)), spread_sem.at[wave])


def transfer(n_py, n_pz, nodal, counts, send_slots, arrival_slots):
    capacity, values = nodal.shape[1:]
    total_slots = n_pz * SLOTS
    elements = total_slots // 2 // BLOCKS
    fourier = jnp.asarray(fourier_table(n_py, elements))
    plane = jnp.asarray(plane_table())
    remote = pl.BlockSpec(memory_space=pltpu.HBM)
    here = functools.partial(pltpu.with_memory_space_constraint, memory_space=pltpu.HBM)
    return pl.pallas_call(
        functools.partial(transfer_kernel, n_py, n_pz),
        out_shape=jax.ShapeDtypeStruct((COMPONENTS, n_py // 8, USED * 16, 128), F32),
        in_specs=[remote] * 6,
        out_specs=pl.BlockSpec(memory_space=pltpu.VMEM),
        scratch_shapes=[
            pltpu.VMEM((COMPONENTS, capacity, values), BF16),
            pltpu.VMEM(counts.shape, jnp.int32),
            pltpu.VMEM(send_slots.shape, jnp.int32),
            pltpu.VMEM(arrival_slots.shape, jnp.int32),
            pltpu.VMEM(fourier.shape, BF16),
            pltpu.VMEM(plane.shape, BF16),
            pltpu.VMEM((total_slots, capacity), BF16),
            pltpu.VMEM((total_slots // 2, total_slots), BF16),
            pltpu.VMEM((COMPONENTS, n_pz, 2, SLOTS, WIDTH), BF16),
            pltpu.VMEM((COMPONENTS, X_RING, 2, SLOTS, WIDTH), BF16),
            pltpu.VMEM((COMPONENTS, n_pz, 2, SLOTS, WIDTH), BF16),
            pltpu.VMEM((NODE * elements, 128), BF16),
            pltpu.VMEM((n_py * TILE, 128), F32),
            pltpu.VMEM((COMPONENTS, n_py, 3, TILE, 128), BF16),
            pltpu.VMEM((COMPONENTS, n_py, 3, TILE, 128), BF16),
            pltpu.SemaphoreType.DMA((8,)),
            *[pltpu.SemaphoreType.DMA((len(WAVES),)) for _ in range(6)],
        ],
        compiler_params=pltpu.CompilerParams(
            collective_id=0, has_side_effects=True, vmem_limit_bytes=40 * 1024 * 1024
        ),
    )(
        here(nodal), counts, here(send_slots), here(arrival_slots), here(fourier), here(plane)
    )


def write_kernel(spectra, out, sem):
    copies = [
        pltpu.make_async_copy(
            spectra.at[c, side], out.at[c, :, pl.ds(side * 128, 128)], sem.at[c, side]
        )
        for c in range(COMPONENTS)
        for side in range(spectra.shape[1])
    ]
    for copy in copies:
        copy.start()
    for copy in copies:
        copy.wait()


def write(spectra):
    sides, rows = spectra.shape[1:3]
    anywhere = pl.BlockSpec(memory_space=pl.ANY)
    return pl.pallas_call(
        write_kernel,
        out_shape=jax.ShapeDtypeStruct((COMPONENTS, rows, sides * 128), F32),
        in_specs=[anywhere],
        out_specs=anywhere,
        scratch_shapes=[pltpu.SemaphoreType.DMA((COMPONENTS, sides))],
        compiler_params=pltpu.CompilerParams(vmem_limit_bytes=40 * 1024 * 1024),
    )(spectra)


def solution(mesh):
    n_py, n_pz = mesh.shape["py"], mesh.shape["pz"]

    def on_device(nodal, element_counts, send_slots, arrival_slots):
        turned = nodal[0].transpose(1, 0, 2)
        spectra = transfer(n_py, n_pz, turned, element_counts, send_slots, arrival_slots)
        return write(spectra).reshape(COMPONENTS, 2, MODES, 16, -1)

    placed = (P("py", "pz", None, None), P("py", "pz"), P("py", "pz"), P("py", "pz"))
    return jax.shard_map(
        on_device,
        mesh=mesh,
        in_specs=placed,
        out_specs=P(None, None, "py", "pz", None),
        check_vma=False,
    )
```

```python
import functools
import math

import jax
import jax.numpy as jnp
import ml_dtypes
import numpy as np
from jax import lax
from jax.experimental import pallas as pl
from jax.experimental.pallas import tpu as pltpu
from jax.sharding import PartitionSpec as P

NODE = 8
YE = 2
LZ = 2
BLOCKS = YE * LZ
COMPONENTS = 3
SLOTS = 16
X_RING = 4
MODES = 10
USED = 2 * MODES
TILE = 16
LEFT = USED - TILE
WAVES = ((0, 0, 2), (1, 0, 2), (2, 0, 1), (2, 1, 1))
PARTS = ((0, 0, 3), (1, 0, 3), (2, 0, 1), (2, 1, 2))
WIDTH = NODE**3 // 2
BF16 = jnp.bfloat16
F32 = jnp.float32
MESH = pl.DeviceIdType.MESH


def lobatto_points(number):
    degree = number - 1
    points = np.cos(np.pi * np.arange(number) / degree)
    for sweeps in range(60):
        older_poly = np.ones(number)
        newer_poly = points.copy()
        for degree_now in range(2, degree + 1):
            older_poly, newer_poly = (
                newer_poly,
                ((2 * degree_now - 1) * points * newer_poly - (degree_now - 1) * older_poly)
                / degree_now,
            )
        points = points - (points * newer_poly - older_poly) / (number * newer_poly)
    return np.sort(points)


def vandermonde(number):
    gauss_points = lobatto_points(number)
    uniform = -1.0 + (2.0 * np.arange(number) + 1.0) / number
    columns_list = []
    for column in range(number):
        same = np.arange(number) == column
        numer = np.where(same[None, :], 1.0, uniform[:, None] - gauss_points[None, :])
        denom = np.where(same, 1.0, gauss_points[column] - gauss_points)
        columns_list.append(np.prod(numer / denom[None, :], axis=1))
    return np.stack(columns_list, axis=1)


def fourier_table(bands, elements):
    length = elements * NODE
    wavenumber = np.arange(bands * MODES)[:, None]
    angles = (wavenumber * np.arange(length)[None, :] % length) * (2.0 * np.pi / length)
    dft = np.stack([np.cos(angles), -np.sin(angles)]) / math.sqrt(length)
    dft = dft.reshape(2, bands, MODES, elements, NODE)
    nodes = np.einsum("tikeh,hn->itkne", dft, vandermonde(NODE))
    nodes = nodes.reshape(bands, USED, NODE, elements)
    table = np.zeros((2, bands, TILE, NODE, elements))
    table[0] = nodes[:, :TILE]
    table[1, :, :LEFT] = nodes[:, TILE:]
    return table.reshape(2 * bands * TILE, NODE * elements).astype(ml_dtypes.bfloat16)


def plane_table():
    lagrange = vandermonde(NODE)
    table = np.einsum("fu,gv,hw->uvhwfg", lagrange, lagrange, np.eye(NODE))
    table = table.reshape(NODE**3, NODE, 2, NODE // 2, NODE).transpose(2, 0, 1, 3, 4)
    return table.reshape(2, NODE**3, NODE**3 // 2).astype(ml_dtypes.bfloat16)


def exchange(tiles, index_bit, lane_bit, width):
    lane = lax.broadcasted_iota(jnp.int32, tiles[0].shape, 1)
    shift = lane_bit * width
    low = lane % (2 * shift) < shift
    turned = list(tiles)
    for at in range(len(tiles)):
        if at & index_bit == 0:
            first, second = tiles[at], tiles[at + index_bit]
            turned[at] = jnp.where(low, first, pltpu.roll(second, shift, 1))
            turned[at + index_bit] = jnp.where(low, pltpu.roll(first, 128 - shift, 1), second)
    return turned


def transfer_kernel(
    n_py, n_pz, nodal, counts, send_slots, arrival_slots, fourier, plane, out,
    nodes, counts_here, send_here, arrival_here, fourier_here, plane_here, pick, place,
    outgoing, arrived, stacked, leftover, coeffs, received,
    load_sem, send_sem, arrive_sem, spread_sem, receive_sem,
):
    me_y = lax.axis_index("py")
    me_z = lax.axis_index("pz")
    z_ring = n_pz // X_RING
    my_plane, my_column = me_z // X_RING, me_z % X_RING
    capacity = nodes.shape[1]
    elements = place.shape[0] // BLOCKS
    total_slots = n_pz * SLOTS

    barrier = pltpu.get_barrier_semaphore()

    def greet_z(step, carry):
        pl.semaphore_signal(
            barrier, inc=1, device_id={"pz": (me_z + step) % n_pz}, device_id_type=MESH
        )
        return carry

    def greet_y(step, carry):
        pl.semaphore_signal(
            barrier, inc=1, device_id={"py": (me_y + step) % n_py}, device_id_type=MESH
        )
        return carry

    pairs = [
        (send_slots, send_here),
        (counts, counts_here),
        (nodal.at[0], nodes.at[0]),
        (plane, plane_here),
        (arrival_slots, arrival_here),
        (nodal.at[1], nodes.at[1]),
        (nodal.at[2], nodes.at[2]),
        (fourier, fourier_here),
    ]
    loads = [
        pltpu.make_async_copy(source, here, load_sem.at[at])
        for at, (source, here) in enumerate(pairs)
    ]
    for load in loads:
        load.start()
    lax.fori_loop(1, n_pz, greet_z, 0)
    lax.fori_loop(1, n_py, greet_y, 0)

    loads[0].wait()
    loads[1].wait()
    column = lax.broadcasted_iota(jnp.int32, (1, capacity), 1)
    target = jnp.where(column < counts_here[...], send_here[...], -1)
    row = lax.broadcasted_iota(jnp.int32, (total_slots, capacity), 0)
    pick[...] = jnp.where(row == target, 1.0, 0.0).astype(BF16)

    def pack(c):
        for half in range(2):
            turned = jnp.dot(nodes[c], plane_here[half], preferred_element_type=F32).astype(BF16)
            packed = jnp.dot(pick[...], turned, preferred_element_type=F32).astype(BF16)
            outgoing[c, :, half] = packed.reshape(n_pz, SLOTS, WIDTH)

    def peer_at(plane_step, column_step):
        peer_plane = (my_plane + plane_step + z_ring) % z_ring
        return peer_plane * X_RING + (my_column + column_step + X_RING) % X_RING

    def block(ref, wave, device):
        c, first, number = WAVES[wave]
        return ref.at[c, device, pl.ds(first, number)]

    def piece(ref, wave, device):
        c, first, number = PARTS[wave]
        return ref.at[c, device, pl.ds(first, number)]

    def wait_for(part, sem):
        pltpu.make_async_copy(part, part, sem).wait()

    def send_to(wave, plane_step, column_step):
        peer = peer_at(plane_step, column_step)
        pltpu.make_async_remote_copy(
            src_ref=block(outgoing, wave, peer),
            dst_ref=block(arrived, wave, me_z),
            send_sem=send_sem.at[wave],
            recv_sem=arrive_sem.at[wave],
            device_id={"pz": peer},
            device_id_type=MESH,
        ).start()

    first_side = 1 - me_y % 2 * 2
    half_ring = z_ring // 2
    far = []
    for p in range((half_ring - 1) * X_RING):
        far += [(side, p % (half_ring - 1) + 1, p % X_RING) for side in (1, -1)]
        if p % (half_ring - 1) == half_ring - 2:
            far.append((1, half_ring, p // (half_ring - 1)))

    def send_far(wave, chosen):
        for side, distance, column in chosen:
            send_to(wave, first_side * side * distance, first_side * side * column)

    def send_near(wave):
        for column in range(1, X_RING):
            send_to(wave, 0, column)
        c, first, number = WAVES[wave]
        for half in range(first, first + number):
            arrived[c, me_z, half] = outgoing[c, me_z, half]

    def send(wave):
        send_near(wave)
        send_far(wave, far)

    def receive(wave):
        wait_for(block(arrived, wave, pl.ds(0, n_pz - 1)), arrive_sem.at[wave])

    def transform(c, half):
        slots = arrived[c, :, half].reshape(total_slots, WIDTH)
        placed = jnp.dot(place[...], slots, preferred_element_type=F32)
        for quad in range(2):
            tiles = [
                placed[at * elements : (at + 1) * elements, quad * 128 : (quad + 1) * 128]
                for at in range(BLOCKS)
            ]
            tiles = exchange(exchange(tiles, 1, 1, 32), 2, 2, 32)
            for at, tile in enumerate(tiles):
                stacked[pl.ds((quad * 4 + at) * elements, elements), :] = tile.astype(BF16)

        result = jnp.dot(fourier_here[...], stacked[...], preferred_element_type=F32)
        main, rest = result[: n_py * TILE], result[n_py * TILE :]
        coeffs[c, :, half] = main.astype(BF16).reshape(n_py, TILE, 128)
        if half == 0:
            leftover[...] = rest
        else:
            both = leftover[...] + pltpu.roll(rest, LEFT, 0)
            coeffs[c, :, 2] = both.astype(BF16).reshape(n_py, TILE, 128)

    def spread(wave):
        c, first, number = PARTS[wave]
        for part in range(first, first + number):
            received[c, me_y, part] = coeffs[c, me_y, part]

        for step in range(1, n_py):
            peer = (me_y + (step + 1) // 2 * (1 - step % 2 * 2) + n_py) % n_py
            pltpu.make_async_remote_copy(
                src_ref=piece(coeffs, wave, peer),
                dst_ref=piece(received, wave, me_y),
                send_sem=spread_sem.at[wave],
                recv_sem=receive_sem.at[wave],
                device_id={"py": peer},
                device_id_type=MESH,
            ).start()

    def gather(wave):
        wait_for(piece(received, wave, pl.ds(0, n_py - 1)), receive_sem.at[wave])

    def put_in_order(c, part):
        def side_step(side, carry):
            tiles = [received[c, side * 8 + band, part].astype(F32) for band in range(8)]
            if part == 2:
                tiles = [tile[: 2 * LEFT] for tile in tiles]
            for index_bit, lane_bit in ((4, 8), (2, 4), (1, 2), (2, 1)):
                tiles = exchange(tiles, index_bit, lane_bit, 8)
            for at in range(8):
                z = at // 4 * 8 + at % 2 * 2 + at // 2 % 2
                if part == 2:
                    for half in range(2):
                        here = pl.ds(TILE * 16 + half * 4 + z, LEFT, stride=16)
                        out[c, side, here, :] = tiles[at][half * LEFT : (half + 1) * LEFT]
                else:
                    out[c, side, pl.ds(part * 4 + z, TILE, stride=16), :] = tiles[at]
            return carry

        lax.fori_loop(0, n_py // 8, side_step, 0)

    loads[2].wait()
    loads[3].wait()
    pack(0)
    pl.semaphore_wait(barrier, n_pz - 1 + n_py - 1)
    send(0)
    loads[5].wait()
    pack(1)
    send(1)
    loads[6].wait()
    pack(2)
    loads[4].wait()
    local = lax.broadcasted_iota(jnp.int32, (place.shape[0], total_slots), 0)
    place[...] = jnp.where(local == arrival_here[...], 1.0, 0.0).astype(BF16)
    loads[7].wait()
    receive(0)
    send(2)
    transform(0, 0)
    transform(0, 1)
    spread(0)
    receive(1)
    transform(1, 0)
    send_near(3)
    send_far(3, far[: len(far) // 2])
    transform(1, 1)
    spread(1)
    send_far(3, far[len(far) // 2 :])
    receive(2)
    transform(2, 0)
    spread(2)
    gather(0)
    for part in range(3):
        put_in_order(0, part)
    receive(3)
    transform(2, 1)
    spread(3)
    gather(1)
    for part in range(3):
        put_in_order(1, part)
    gather(2)
    put_in_order(2, 0)
    gather(3)
    put_in_order(2, 1)
    put_in_order(2, 2)
    for wave in range(len(WAVES)):
        wait_for(block(outgoing, wave, pl.ds(0, n_pz - 1)), send_sem.at[wave])
        wait_for(piece(coeffs, wave, pl.ds(0, n_py - 1)), spread_sem.at[wave])


def transfer(n_py, n_pz, nodal, counts, send_slots, arrival_slots):
    capacity, values = nodal.shape[1:]
    total_slots = n_pz * SLOTS
    elements = total_slots // 2 // BLOCKS
    fourier = jnp.asarray(fourier_table(n_py, elements))
    plane = jnp.asarray(plane_table())
    remote = pl.BlockSpec(memory_space=pltpu.HBM)
    here = functools.partial(pltpu.with_memory_space_constraint, memory_space=pltpu.HBM)
    return pl.pallas_call(
        functools.partial(transfer_kernel, n_py, n_pz),
        out_shape=jax.ShapeDtypeStruct((COMPONENTS, n_py // 8, USED * 16, 128), F32),
        in_specs=[remote] * 6,
        out_specs=pl.BlockSpec(memory_space=pltpu.VMEM),
        scratch_shapes=[
            pltpu.VMEM((COMPONENTS, capacity, values), BF16),
            pltpu.VMEM(counts.shape, jnp.int32),
            pltpu.VMEM(send_slots.shape, jnp.int32),
            pltpu.VMEM(arrival_slots.shape, jnp.int32),
            pltpu.VMEM(fourier.shape, BF16),
            pltpu.VMEM(plane.shape, BF16),
            pltpu.VMEM((total_slots, capacity), BF16),
            pltpu.VMEM((total_slots // 2, total_slots), BF16),
            pltpu.VMEM((COMPONENTS, n_pz, 2, SLOTS, WIDTH), BF16),
            pltpu.VMEM((COMPONENTS, n_pz, 2, SLOTS, WIDTH), BF16),
            pltpu.VMEM((NODE * elements, 128), BF16),
            pltpu.VMEM((n_py * TILE, 128), F32),
            pltpu.VMEM((COMPONENTS, n_py, 3, TILE, 128), BF16),
            pltpu.VMEM((COMPONENTS, n_py, 3, TILE, 128), BF16),
            pltpu.SemaphoreType.DMA((8,)),
            *[pltpu.SemaphoreType.DMA((len(WAVES),)) for _ in range(4)],
        ],
        compiler_params=pltpu.CompilerParams(
            collective_id=0, has_side_effects=True, vmem_limit_bytes=40 * 1024 * 1024
        ),
    )(
        here(nodal), counts, here(send_slots), here(arrival_slots), here(fourier), here(plane)
    )


def write_kernel(spectra, out, sem):
    copies = [
        pltpu.make_async_copy(
            spectra.at[c, side], out.at[c, :, pl.ds(side * 128, 128)], sem.at[c, side]
        )
        for c in range(COMPONENTS)
        for side in range(spectra.shape[1])
    ]
    for copy in copies:
        copy.start()
    for copy in copies:
        copy.wait()


def write(spectra):
    sides, rows = spectra.shape[1:3]
    anywhere = pl.BlockSpec(memory_space=pl.ANY)
    return pl.pallas_call(
        write_kernel,
        out_shape=jax.ShapeDtypeStruct((COMPONENTS, rows, sides * 128), F32),
        in_specs=[anywhere],
        out_specs=anywhere,
        scratch_shapes=[pltpu.SemaphoreType.DMA((COMPONENTS, sides))],
        compiler_params=pltpu.CompilerParams(vmem_limit_bytes=40 * 1024 * 1024),
    )(spectra)


def solution(mesh):
    n_py, n_pz = mesh.shape["py"], mesh.shape["pz"]

    def on_device(nodal, element_counts, send_slots, arrival_slots):
        turned = nodal[0].transpose(1, 0, 2)
        spectra = transfer(n_py, n_pz, turned, element_counts, send_slots, arrival_slots)
        return write(spectra).reshape(COMPONENTS, 2, MODES, 16, -1)

    placed = (P("py", "pz", None, None), P("py", "pz"), P("py", "pz"), P("py", "pz"))
    return jax.shard_map(
        on_device,
        mesh=mesh,
        in_specs=placed,
        out_specs=P(None, None, "py", "pz", None),
        check_vma=False,
    )
```

```python
import functools
import math

import jax
import jax.numpy as jnp
import ml_dtypes
import numpy as np
from jax import lax
from jax.experimental import pallas as pl
from jax.experimental.pallas import tpu as pltpu
from jax.sharding import PartitionSpec as P

NODE = 8
YE = 2
LZ = 2
BLOCKS = YE * LZ
COMPONENTS = 3
SLOTS = 16
X_RING = 4
MODES = 10
USED = 2 * MODES
TILE = 16
LEFT = USED - TILE
GROUP = 8
WAVES = ((0, 0, 2), (1, 0, 2), (2, 0, 1), (2, 1, 1))
PARTS = ((0, 0, 3), (1, 0, 3), (2, 0, 1), (2, 1, 2))
WIDTH = NODE**3 // 2
BF16 = jnp.bfloat16
F32 = jnp.float32
MESH = pl.DeviceIdType.MESH


def lobatto_points(number):
    degree = number - 1
    points = np.cos(np.pi * np.arange(number) / degree)
    for sweeps in range(60):
        older_poly = np.ones(number)
        newer_poly = points.copy()
        for degree_now in range(2, degree + 1):
            older_poly, newer_poly = (
                newer_poly,
                ((2 * degree_now - 1) * points * newer_poly - (degree_now - 1) * older_poly)
                / degree_now,
            )
        points = points - (points * newer_poly - older_poly) / (number * newer_poly)
    return np.sort(points)


def vandermonde(number):
    gauss_points = lobatto_points(number)
    uniform = -1.0 + (2.0 * np.arange(number) + 1.0) / number
    columns_list = []
    for column in range(number):
        same = np.arange(number) == column
        numer = np.where(same[None, :], 1.0, uniform[:, None] - gauss_points[None, :])
        denom = np.where(same, 1.0, gauss_points[column] - gauss_points)
        columns_list.append(np.prod(numer / denom[None, :], axis=1))
    return np.stack(columns_list, axis=1)


def fourier_table(bands, elements):
    length = elements * NODE
    wavenumber = np.arange(bands * MODES)[:, None]
    angles = (wavenumber * np.arange(length)[None, :] % length) * (2.0 * np.pi / length)
    dft = np.stack([np.cos(angles), -np.sin(angles)]) / math.sqrt(length)
    dft = dft.reshape(2, bands, MODES, elements, NODE)
    nodes = np.einsum("tikeh,hn->itkne", dft, vandermonde(NODE))
    nodes = nodes.reshape(bands, USED, NODE, elements)
    table = np.zeros((2, bands, TILE, NODE, elements))
    table[0] = nodes[:, :TILE]
    table[1, :, :LEFT] = nodes[:, TILE:]
    return table.reshape(2, bands * TILE, NODE * elements).astype(ml_dtypes.bfloat16)


def plane_table():
    lagrange = vandermonde(NODE)
    table = np.einsum("fu,gv,hw->uvhwfg", lagrange, lagrange, np.eye(NODE))
    table = table.reshape(NODE**3, NODE, 2, NODE // 2, NODE).transpose(2, 0, 1, 3, 4)
    return table.reshape(2, NODE**3, NODE**3 // 2).astype(ml_dtypes.bfloat16)


def exchange(tiles, index_bit, lane_bit, width):
    lane = lax.broadcasted_iota(jnp.int32, tiles[0].shape, 1)
    shift = lane_bit * width
    low = lane % (2 * shift) < shift
    turned = list(tiles)
    for at in range(len(tiles)):
        if at & index_bit == 0:
            first, second = tiles[at], tiles[at + index_bit]
            turned[at] = jnp.where(low, first, pltpu.roll(second, shift, 1))
            turned[at + index_bit] = jnp.where(low, pltpu.roll(first, 128 - shift, 1), second)
    return turned


def transfer_kernel(
    n_py, n_pz, nodal, counts, send_slots, arrival_slots, fourier, plane, out,
    nodes, counts_here, send_here, arrival_here, fourier_here, plane_here, pick, place,
    outgoing, relayed, arrived, stacked, leftover, coeffs, received,
    load_sem, send_sem, relay_sem, forward_sem, arrive_sem, spread_sem, receive_sem,
):
    me_y = lax.axis_index("py")
    me_z = lax.axis_index("pz")
    z_ring = n_pz // X_RING
    my_plane, my_column = me_z // X_RING, me_z % X_RING
    capacity = nodes.shape[1]
    elements = place.shape[0] // BLOCKS
    total_slots = n_pz * SLOTS

    barrier = pltpu.get_barrier_semaphore()

    def greet_z(step, carry):
        pl.semaphore_signal(
            barrier, inc=1, device_id={"pz": (me_z + step) % n_pz}, device_id_type=MESH
        )
        return carry

    def greet_y(step, carry):
        pl.semaphore_signal(
            barrier, inc=1, device_id={"py": (me_y + step) % n_py}, device_id_type=MESH
        )
        return carry

    pairs = [
        (send_slots, send_here),
        (counts, counts_here),
        (nodal.at[0], nodes.at[0]),
        (plane, plane_here),
        (arrival_slots, arrival_here),
        (nodal.at[1], nodes.at[1]),
        (nodal.at[2], nodes.at[2]),
        (fourier, fourier_here),
    ]
    loads = [
        pltpu.make_async_copy(source, here, load_sem.at[at])
        for at, (source, here) in enumerate(pairs)
    ]
    for load in loads[:4]:
        load.start()
    lax.fori_loop(1, n_pz, greet_z, 0)
    lax.fori_loop(1, n_py, greet_y, 0)

    loads[0].wait()
    loads[1].wait()
    column = lax.broadcasted_iota(jnp.int32, (1, capacity), 1)
    target = jnp.where(column < counts_here[...], send_here[...], -1)
    row = lax.broadcasted_iota(jnp.int32, (total_slots, capacity), 0)
    pick[...] = jnp.where(row == target, 1.0, 0.0).astype(BF16)

    def pack(c, halves=(0, 1)):
        for half in halves:
            turned = jnp.dot(nodes[c], plane_here[half], preferred_element_type=F32).astype(BF16)
            packed = jnp.dot(pick[...], turned, preferred_element_type=F32).astype(BF16)
            outgoing[c, :, half] = packed.reshape(n_pz, SLOTS, WIDTH)

    def peer_at(plane_step, column_step):
        peer_plane = (my_plane + plane_step + z_ring) % z_ring
        return peer_plane * X_RING + (my_column + column_step + X_RING) % X_RING

    def block(ref, wave, device, span=None):
        c, first, number = WAVES[wave]
        first, number = span or (first, number)
        return ref.at[c, device, pl.ds(first, number)]

    def piece(ref, wave, device):
        c, first, number = PARTS[wave]
        return ref.at[c, device, pl.ds(first, number)]

    def wait_for(part, sem):
        pltpu.make_async_copy(part, part, sem).wait()

    def send_to(wave, plane_step, column_step, span):
        peer = peer_at(plane_step, column_step)
        pltpu.make_async_remote_copy(
            src_ref=block(outgoing, wave, peer, span),
            dst_ref=block(arrived, wave, me_z, span),
            send_sem=send_sem.at[wave],
            recv_sem=arrive_sem.at[wave],
            device_id={"pz": peer},
            device_id_type=MESH,
        ).start()

    quarter = z_ring // 4

    def send_opposite(wave, span=None):
        def opposite(step, carry):
            way = (1 - step % 2 * 2) * quarter
            pltpu.make_async_remote_copy(
                src_ref=block(outgoing, wave, peer_at(2 * quarter, step), span),
                dst_ref=block(relayed, wave, step, span),
                send_sem=send_sem.at[wave],
                recv_sem=relay_sem.at[wave],
                device_id={"pz": peer_at(way, step)},
                device_id_type=MESH,
            ).start()
            return carry

        lax.fori_loop(0, X_RING, opposite, 0)

    def send(wave, span=None):
        def far(step, carry):
            side = 1 - (step + me_y) % 2 * 2
            pair = step // 2
            send_to(wave, side * (pair % (z_ring // 2 - 1) + 1), side * (pair % X_RING), span)
            return carry

        def near(step, carry):
            send_to(wave, 0, step, span)
            return carry

        lax.fori_loop(1, X_RING, near, 0)
        lax.fori_loop(0, (z_ring - 2) * X_RING, far, 0)
        c, first, number = WAVES[wave]
        first, number = span or (first, number)
        for half in range(first, first + number):
            arrived[c, me_z, half] = outgoing[c, me_z, half]

    def forward(wave):
        wait_for(block(relayed, wave, pl.ds(0, X_RING)), relay_sem.at[wave])

        def onward(step, carry):
            way = (1 - step % 2 * 2) * quarter
            pltpu.make_async_remote_copy(
                src_ref=block(relayed, wave, step),
                dst_ref=block(arrived, wave, peer_at(-way, -step)),
                send_sem=forward_sem.at[wave],
                recv_sem=arrive_sem.at[wave],
                device_id={"pz": peer_at(way, 0)},
                device_id_type=MESH,
            ).start()
            return carry

        lax.fori_loop(0, X_RING, onward, 0)

    def receive(wave):
        wait_for(block(arrived, wave, pl.ds(0, n_pz - 1)), arrive_sem.at[wave])

    rows = GROUP * TILE
    groups = n_py // GROUP

    def transform(c, half):
        slots = arrived[c, :, half].reshape(total_slots, WIDTH)
        placed = jnp.dot(place[...], slots, preferred_element_type=F32)
        for quad in range(2):
            tiles = [
                placed[at * elements : (at + 1) * elements, quad * 128 : (quad + 1) * 128]
                for at in range(BLOCKS)
            ]
            tiles = exchange(exchange(tiles, 1, 1, 32), 2, 2, 32)
            for at, tile in enumerate(tiles):
                stacked[pl.ds((quad * 4 + at) * elements, elements), :] = tile.astype(BF16)

        def group_step(step, carry):
            here = pl.ds(pl.multiple_of(step * rows, rows), rows)
            members = pl.ds(step * GROUP, GROUP)
            result = jnp.dot(fourier_here[0, here], stacked[...], preferred_element_type=F32)
            coeffs[c, members, half] = result.astype(BF16).reshape(GROUP, TILE, 128)
            rest = jnp.dot(fourier_here[1, here], stacked[...], preferred_element_type=F32)
            if half == 0:
                leftover[here] = rest
            else:
                both = leftover[here] + pltpu.roll(rest, LEFT, 0)
                coeffs[c, members, 2] = both.astype(BF16).reshape(GROUP, TILE, 128)
            return carry

        lax.fori_loop(0, groups, group_step, 0)

    def spread(wave):
        c, first, number = PARTS[wave]
        for part in range(first, first + number):
            received[c, me_y, part] = coeffs[c, me_y, part]

        def spread_to(step, carry):
            peer = (me_y + (step + 1) // 2 * (1 - step % 2 * 2) + n_py) % n_py
            pltpu.make_async_remote_copy(
                src_ref=piece(coeffs, wave, peer),
                dst_ref=piece(received, wave, me_y),
                send_sem=spread_sem.at[wave],
                recv_sem=receive_sem.at[wave],
                device_id={"py": peer},
                device_id_type=MESH,
            ).start()
            return carry

        lax.fori_loop(1, n_py, spread_to, 0)

    def gather(wave):
        wait_for(piece(received, wave, pl.ds(0, n_py - 1)), receive_sem.at[wave])

    def put_in_order(c, part):
        def side_step(side, carry):
            tiles = [received[c, side * 8 + band, part].astype(F32) for band in range(8)]
            if part == 2:
                tiles = [tile[: 2 * LEFT] for tile in tiles]
            for index_bit, lane_bit in ((4, 8), (2, 4), (1, 2), (2, 1)):
                tiles = exchange(tiles, index_bit, lane_bit, 8)
            for at in range(8):
                z = at // 4 * 8 + at % 2 * 2 + at // 2 % 2
                if part == 2:
                    for half in range(2):
                        here = pl.ds(TILE * 16 + half * 4 + z, LEFT, stride=16)
                        out[c, side, here, :] = tiles[at][half * LEFT : (half + 1) * LEFT]
                else:
                    out[c, side, pl.ds(part * 4 + z, TILE, stride=16), :] = tiles[at]
            return carry

        lax.fori_loop(0, n_py // 8, side_step, 0)

    loads[2].wait()
    loads[3].wait()
    pack(0, (0,))
    pl.semaphore_wait(barrier, n_pz - 1 + n_py - 1)
    send_opposite(0, (0, 1))
    send(0, (0, 1))
    for load in loads[4:]:
        load.start()
    pack(0, (1,))
    send_opposite(0, (1, 1))
    send(0, (1, 1))
    loads[5].wait()
    pack(1)
    send_opposite(1)
    forward(0)
    send(1)
    loads[6].wait()
    pack(2)
    send_opposite(2)
    send_opposite(3)
    loads[4].wait()
    local = lax.broadcasted_iota(jnp.int32, (place.shape[0], total_slots), 0)
    place[...] = jnp.where(local == arrival_here[...], 1.0, 0.0).astype(BF16)
    loads[7].wait()
    forward(1)
    receive(0)
    send(2)
    transform(0, 0)
    transform(0, 1)
    spread(0)
    receive(1)
    forward(2)
    forward(3)
    transform(1, 0)
    transform(1, 1)
    spread(1)
    send(3)
    receive(2)
    transform(2, 0)
    spread(2)
    gather(0)
    for part in range(3):
        put_in_order(0, part)
    receive(3)
    transform(2, 1)
    spread(3)
    gather(1)
    for part in range(3):
        put_in_order(1, part)
    gather(2)
    put_in_order(2, 0)
    gather(3)
    put_in_order(2, 1)
    put_in_order(2, 2)
    for wave in range(len(WAVES)):
        wait_for(block(outgoing, wave, pl.ds(0, n_pz - 1)), send_sem.at[wave])
        wait_for(block(relayed, wave, pl.ds(0, X_RING)), forward_sem.at[wave])
        wait_for(piece(coeffs, wave, pl.ds(0, n_py - 1)), spread_sem.at[wave])


def transfer(n_py, n_pz, nodal, counts, send_slots, arrival_slots):
    capacity, values = nodal.shape[1:]
    total_slots = n_pz * SLOTS
    elements = total_slots // 2 // BLOCKS
    fourier = jnp.asarray(fourier_table(n_py, elements))
    plane = jnp.asarray(plane_table())
    remote = pl.BlockSpec(memory_space=pltpu.HBM)
    here = functools.partial(pltpu.with_memory_space_constraint, memory_space=pltpu.HBM)
    return pl.pallas_call(
        functools.partial(transfer_kernel, n_py, n_pz),
        out_shape=jax.ShapeDtypeStruct((COMPONENTS, n_py // 8, USED * 16, 128), F32),
        in_specs=[remote] * 6,
        out_specs=pl.BlockSpec(memory_space=pltpu.VMEM),
        scratch_shapes=[
            pltpu.VMEM((COMPONENTS, capacity, values), BF16),
            pltpu.VMEM(counts.shape, jnp.int32),
            pltpu.VMEM(send_slots.shape, jnp.int32),
            pltpu.VMEM(arrival_slots.shape, jnp.int32),
            pltpu.VMEM(fourier.shape, BF16),
            pltpu.VMEM(plane.shape, BF16),
            pltpu.VMEM((total_slots, capacity), BF16),
            pltpu.VMEM((total_slots // 2, total_slots), BF16),
            pltpu.VMEM((COMPONENTS, n_pz, 2, SLOTS, WIDTH), BF16),
            pltpu.VMEM((COMPONENTS, X_RING, 2, SLOTS, WIDTH), BF16),
            pltpu.VMEM((COMPONENTS, n_pz, 2, SLOTS, WIDTH), BF16),
            pltpu.VMEM((NODE * elements, 128), BF16),
            pltpu.VMEM((n_py * TILE, 128), F32),
            pltpu.VMEM((COMPONENTS, n_py, 3, TILE, 128), BF16),
            pltpu.VMEM((COMPONENTS, n_py, 3, TILE, 128), BF16),
            pltpu.SemaphoreType.DMA((8,)),
            *[pltpu.SemaphoreType.DMA((len(WAVES),)) for _ in range(6)],
        ],
        compiler_params=pltpu.CompilerParams(
            collective_id=0, has_side_effects=True, vmem_limit_bytes=40 * 1024 * 1024
        ),
    )(
        here(nodal), counts, here(send_slots), here(arrival_slots), here(fourier), here(plane)
    )


def write_kernel(spectra, out, sem):
    copies = [
        pltpu.make_async_copy(
            spectra.at[c, side], out.at[c, :, pl.ds(side * 128, 128)], sem.at[c, side]
        )
        for c in range(COMPONENTS)
        for side in range(spectra.shape[1])
    ]
    for copy in copies:
        copy.start()
    for copy in copies:
        copy.wait()


def write(spectra):
    sides, rows = spectra.shape[1:3]
    anywhere = pl.BlockSpec(memory_space=pl.ANY)
    return pl.pallas_call(
        write_kernel,
        out_shape=jax.ShapeDtypeStruct((COMPONENTS, rows, sides * 128), F32),
        in_specs=[anywhere],
        out_specs=anywhere,
        scratch_shapes=[pltpu.SemaphoreType.DMA((COMPONENTS, sides))],
        compiler_params=pltpu.CompilerParams(vmem_limit_bytes=40 * 1024 * 1024),
    )(spectra)


def solution(mesh):
    n_py, n_pz = mesh.shape["py"], mesh.shape["pz"]

    def on_device(nodal, element_counts, send_slots, arrival_slots):
        turned = nodal[0].transpose(1, 0, 2)
        spectra = transfer(n_py, n_pz, turned, element_counts, send_slots, arrival_slots)
        return write(spectra).reshape(COMPONENTS, 2, MODES, 16, -1)

    placed = (P("py", "pz", None, None), P("py", "pz"), P("py", "pz"), P("py", "pz"))
    return jax.shard_map(
        on_device,
        mesh=mesh,
        in_specs=placed,
        out_specs=P(None, None, "py", "pz", None),
        check_vma=False,
    )
```
